256 devices in a mesh: dp: 32 (over z, x_lo, core), expert: 8 (over x_hi, y).
Axes of the slice: x: 4 (x_hi: 2, x_lo: 2; x = x_hi * 2 + x_lo), y: 4, z: 8, core: 2. Of those that a mesh axis runs over, the one named last changes fastest.
Arguments:
- tokens: bfloat16 [4096, 2048], P('dp'), may hold values from -6 to 6
- expert_ids: int32 [4096, 8], P('dp'), may hold values from 0 to 127, all different within a row; in each aligned block of 128 rows (0 to 127, 128 to 255, ...) at most 16 rows name the same one
- route_weight: float32 [4096, 8], P('dp'), may hold values from 0.05 to 0.6
- expert_slot: int32 [128], replicated, may hold values from 0 to 127, each once
- gate_weight: bfloat16 [256, 2048, 384], P(('dp', 'expert')), may hold values from -0.125 to 0.125
- up_weight: bfloat16 [256, 2048, 384], P(('dp', 'expert')), may hold values from -0.125 to 0.125
- down_weight: bfloat16 [256, 384, 2048], P(('dp', 'expert')), may hold values from -0.21875 to 0.21875
- cotangent: bfloat16 [4096, 2048], P('dp'), may hold values from -6 to 6
Outputs:
- layer_out: bfloat16 [4096, 2048], P(('dp', 'expert'))
- input_grad: bfloat16 [4096, 2048], P(('dp', 'expert'))
- gate_grad: bfloat16 [256, 2048, 384], P(('dp', 'expert'))
- up_grad: bfloat16 [256, 2048, 384], P(('dp', 'expert'))
- down_grad: bfloat16 [256, 384, 2048], P(('dp', 'expert'))
The draws below stay inside these ranges and needn't reach their ends.
Inputs may be any that keep to these rules, and one draw needn't show every extreme that they name: `expert_ids`: each token names 8 different experts; among the 128 tokens of one dp index (aligned blocks of rows) no expert is named more than 16 times, and in some or all blocks one expert is named exactly 16 times. A permutation: the expert e sits in slot expert_slot[e].
All inputs are finite; a program needn't handle non-finite values.
Results may differ from the reference program's by a relative error of at most 0.0058.
Values may be sent and summed in bfloat16 or wider, within the bound.
No kernel may reach another device: no remote copies, remote signals or barrier semaphores. Data moves between devices by JAX's collectives and lax.ppermute only.
A program may use at most 128 MiB of HBM per device.

```python
import math
import jax
import jax.numpy as jnp
import numpy as np
from jax import lax

D = 2048
FF = 768
TOPK = 8
TOK_DP = 128
EXPERTS = 128
CAP = 16
TOKENS = 4096
N_DP = 32


def block_levels(stream_key, extent, split, low, high):
    gain, own = 1.0, jax.random.fold_in(stream_key, 6)
    for dim, parts in split:
        steps = jnp.exp(jax.random.uniform(jax.random.fold_in(own, dim), (parts,), jnp.float32, low / len(split), high / len(split)))
        gain = gain * jnp.repeat(steps, extent[dim] // parts).reshape([-1 if axis == dim else 1 for axis in range(len(extent))])
    return gain


def deal_out(stream_key, own, number, rows, count, top, most, skew):
    ranking = jax.random.permutation(stream_key, count)
    heavy_load, common = load_shares(count, rows * top, most, skew, True), load_shares(count, rows * top, most, skew, False)
    places = jnp.arange(count)

    def named(lengths, rotation):
        used = int((lengths > 0).sum())
        fixed = max(1, used // 4)
        moved = fixed + (places - fixed + rotation * (used - fixed)) % max(1, count - fixed)
        return jnp.zeros((count,), jnp.int32).at[ranking[jnp.where(places < fixed, places, moved)]].set(jnp.asarray(lengths, jnp.int32))

    lengths = jnp.where(number % 4 == 0, named(heavy_load, number // 4), named(common, number - number // 4 - 1))
    mixed = jax.random.permutation(jax.random.fold_in(own, 3), count)
    donor, taker = mixed[0:count // 2 * 2:2], mixed[1:count // 2 * 2:2]
    slack = jnp.minimum(lengths[donor] - 1, most - lengths[taker]) // 2
    slack = jnp.where((donor == ranking[0]) | (taker == ranking[0]) | (lengths[taker] == 0), 0, jnp.maximum(slack, 0))
    moved = jax.random.randint(jax.random.fold_in(own, 4), (count // 2,), 0, 1 << 20) % (slack + 1)
    lengths = lengths.at[donor].add(-moved).at[taker].add(moved)
    members = jnp.searchsorted(jnp.cumsum(lengths), jnp.arange(rows * top), side="right").astype(jnp.int32)
    grid = members.reshape(top, rows).T
    grid = grid[jax.random.permutation(jax.random.fold_in(own, 1), rows)]
    rotation = jax.random.randint(jax.random.fold_in(own, 2), (rows, 1), 0, top)
    return jnp.take_along_axis(grid, (jnp.arange(top)[None, :] + rotation) % top, axis=1)


def load_shares(number_of, total, limit, lean, full):
    portions = [(1 << 20) // math.isqrt(grade ** lean) + 1 for grade in range(1, number_of + 1)]
    largest = limit if full else min(limit, max(-(-total // number_of), total * portions[0] // sum(portions)))
    least = 1 if total - largest >= number_of - 1 else 0
    given, rest = [largest] + [least] * (number_of - 1), total - largest - least * (number_of - 1)
    while rest > 0:
        free = [i for i in range(1, number_of) if given[i] < largest] or [i for i in range(1, number_of) if given[i] < limit]
        pool, left = sum([portions[i] for i in free]), rest
        for i in free:
            addition = min(limit - given[i], max(1, left * portions[i] // pool), rest)
            given[i] = given[i] + addition
            rest = rest - addition
    return np.array(given)


def bell_draw(key, shape, width, most, split=(), held_as=jnp.bfloat16):
    array = width * jax.random.normal(key, shape, jnp.float32)
    if split:
        array = array * block_levels(key, shape, split, -0.22, 0.18)
    return jnp.clip(array, -most, most).astype(held_as)


def setup_inputs(seed: int = 0) -> dict:
    splits = jax.random.split(jax.random.key(seed), 9)
    tokens = bell_draw(splits[0], (TOKENS, D), 1.0, 6.0, ((0, 32),))
    expert_ids_keys = jax.random.split(jax.random.fold_in(splits[1], 1), TOKENS // TOK_DP)
    expert_ids_turns = jax.random.permutation(jax.random.fold_in(splits[1], 3), TOKENS // TOK_DP)
    expert_ids = jax.vmap(lambda own, number: deal_out(jax.random.fold_in(splits[1], 2), own, number, TOK_DP, EXPERTS, TOPK, CAP, 2))(expert_ids_keys, expert_ids_turns).reshape((TOKENS, TOPK))
    route_weight = jnp.clip(0.05 + 0.55 * jax.random.uniform(splits[2], (TOKENS, TOPK), jnp.float32) ** block_levels(splits[2], (TOKENS, TOPK), ((0, 32),), -0.2, 0.2), 0.05, 0.6)
    expert_slot = jax.random.permutation(splits[3], EXPERTS).astype(jnp.int32)
    gate_weight = bell_draw(splits[4], (2 * EXPERTS, D, FF // 2), D ** -0.5, 0.125, ((0, 256),))
    up_weight = bell_draw(splits[5], (2 * EXPERTS, D, FF // 2), D ** -0.5, 0.125, ((0, 256),))
    down_weight = bell_draw(splits[6], (2 * EXPERTS, FF // 2, D), FF ** -0.5, 0.21875, ((0, 256),))
    cotangent = bell_draw(splits[7], (TOKENS, D), 1.0, 6.0, ((0, 32),))
    return dict(tokens=tokens, expert_ids=expert_ids, route_weight=route_weight, expert_slot=expert_slot, gate_weight=gate_weight, up_weight=up_weight, down_weight=down_weight, cotangent=cotangent)


def half_expert(x_rows, scaled_rows, w_gate, w_up, w_down):
    gate_val = jnp.dot(x_rows, w_gate, preferred_element_type=jnp.float32)
    up_val = jnp.dot(x_rows, w_up, preferred_element_type=jnp.float32)
    sigma_val = jax.nn.sigmoid(gate_val)
    act_val = gate_val * sigma_val
    hidden = (act_val * up_val).astype(jnp.bfloat16)
    out_part = jnp.dot(hidden, w_down, preferred_element_type=jnp.float32)
    returned = lax.dot_general(scaled_rows, w_down, (((1,), (1,)), ((), ())), preferred_element_type=jnp.float32)
    d_gate = (returned * up_val * sigma_val * (1.0 + gate_val * (1.0 - sigma_val))).astype(jnp.bfloat16)
    d_up = (returned * act_val).astype(jnp.bfloat16)
    grad_down = lax.dot_general(hidden, scaled_rows, (((0,), (0,)), ((), ())), preferred_element_type=jnp.float32).astype(jnp.bfloat16)
    grad_gate = lax.dot_general(x_rows, d_gate, (((0,), (0,)), ((), ())), preferred_element_type=jnp.float32).astype(jnp.bfloat16)
    grad_up = lax.dot_general(x_rows, d_up, (((0,), (0,)), ((), ())), preferred_element_type=jnp.float32).astype(jnp.bfloat16)
    first_term = lax.dot_general(d_gate, w_gate, (((1,), (1,)), ((), ())), preferred_element_type=jnp.float32)
    second_term = lax.dot_general(d_up, w_up, (((1,), (1,)), ((), ())), preferred_element_type=jnp.float32)
    in_piece = first_term + second_term
    return out_part, in_piece, grad_gate, grad_up, grad_down


def reference(tokens, expert_ids, route_weight, expert_slot, gate_weight, up_weight, down_weight, cotangent):
    tok_total = tokens.shape[0]
    flat_slot = expert_slot[expert_ids.reshape(-1)].astype(jnp.int32)
    flat_tok = (jnp.arange(tok_total * TOPK, dtype=jnp.int32) // TOPK).astype(jnp.int32)
    flat_weight = route_weight.reshape(-1)
    sorted_at = jnp.argsort(flat_slot, stable=True).astype(jnp.int32)
    expert_table = jnp.arange(EXPERTS, dtype=jnp.int32)
    counts = jnp.sum((flat_slot[:, None] == expert_table[None, :]).astype(jnp.int32), axis=0).astype(jnp.int32)
    starts = (jnp.cumsum(counts) - counts).astype(jnp.int32)
    most_rows = N_DP * CAP
    padded_at = jnp.concatenate([sorted_at, jnp.zeros((most_rows,), jnp.int32)])
    gates = gate_weight.reshape(EXPERTS, 2, D, FF // 2)
    ups = up_weight.reshape(EXPERTS, 2, D, FF // 2)
    downs = down_weight.reshape(EXPERTS, 2, FF // 2, D)

    def slot_step(carried, inputs):
        out_acc, grad_acc = carried
        slot_idx, w_gate, w_up, w_down = inputs
        picked = lax.dynamic_slice_in_dim(padded_at, starts[slot_idx], most_rows).astype(jnp.int32)
        is_valid = jnp.arange(most_rows, dtype=jnp.int32) < counts[slot_idx]
        rows_tok = flat_tok[picked]
        weight = jnp.where(is_valid, flat_weight[picked], jnp.zeros((), flat_weight.dtype))
        x_rows = jnp.where(is_valid[:, None], tokens[rows_tok], jnp.zeros((), tokens.dtype))
        scaled_rows = (weight[:, None] * cotangent[rows_tok].astype(jnp.float32)).astype(jnp.bfloat16)
        first_half = half_expert(x_rows, scaled_rows, w_gate[0], w_up[0], w_down[0])
        second_half = half_expert(x_rows, scaled_rows, w_gate[1], w_up[1], w_down[1])
        mixed_rows = weight[:, None] * (first_half[0] + second_half[0])
        grad_rows = jnp.where(is_valid[:, None], first_half[1] + second_half[1], jnp.zeros((), jnp.float32))
        out_acc = out_acc.at[rows_tok].add(mixed_rows)
        grad_acc = grad_acc.at[rows_tok].add(grad_rows)
        grad_parts = (jnp.stack([first_half[2], second_half[2]]), jnp.stack([first_half[3], second_half[3]]), jnp.stack([first_half[4], second_half[4]]))
        return (out_acc, grad_acc), grad_parts

    start_acc = jnp.zeros((tok_total, D), jnp.float32)
    (out_acc, grad_acc), grad_parts = lax.scan(slot_step, (start_acc, start_acc), (expert_table, gates, ups, downs))
    gate_grad = grad_parts[0].reshape(2 * EXPERTS, D, FF // 2)
    up_grad = grad_parts[1].reshape(2 * EXPERTS, D, FF // 2)
    down_grad = grad_parts[2].reshape(2 * EXPERTS, FF // 2, D)
    return out_acc.astype(jnp.bfloat16), grad_acc.astype(jnp.bfloat16), gate_grad, up_grad, down_grad
```

```python
import jax
import jax.numpy as jnp
from jax import lax
from jax.experimental import pallas as pl
from jax.experimental.pallas import tpu as pltpu
from jax.sharding import Mesh, PartitionSpec as P

DP = ("z", "xl", "core")
EX = ("xh", "y")
PLANE = ("xl", "core", "xh", "y")
BF16 = jnp.bfloat16
F32 = jnp.float32
CAP = 16
META = 16


def nn(a, b):
    return lax.dot_general(a, b, (((1,), (0,)), ((), ())), preferred_element_type=F32)


def nt(a, b):
    return lax.dot_general(a, b, (((1,), (1,)), ((), ())), preferred_element_type=F32)


def tn(a, b):
    return lax.dot_general(a, b, (((0,), (0,)), ((), ())), preferred_element_type=F32)


def params(mib=48):
    return pltpu.CompilerParams(vmem_limit_bytes=mib * 2**20)


def whole(shape):
    return pl.BlockSpec(shape, lambda *_: (0,) * len(shape))


def route_kernel(col_ref, tok_ref, cot_ref, ids_ref, rw_ref, slot_ref, x_ref, g_ref):
    ntok = tok_ref.shape[0]
    x_ref[0:ntok, :] = tok_ref[...]
    g_ref[...] = cot_ref[...]
    table = jnp.broadcast_to(slot_ref[...], (8, slot_ref.shape[1]))
    slots = jnp.take_along_axis(table, ids_ref[...], axis=1, mode="promise_in_bounds").astype(F32)
    w = rw_ref[...]
    hi = w.astype(BF16).astype(F32)
    rest = w - hi
    mid = rest.astype(BF16).astype(F32)
    low = rest - mid
    left = jnp.concatenate([slots, mid], axis=0)
    right = jnp.concatenate([hi, low], axis=0)
    x_ref[ntok : ntok + META, 0:128] = left.astype(BF16)
    x_ref[ntok : ntok + META, 128:256] = right.astype(BF16)


def route(col, tokens, cotangent, ids_t, rw_t, slot_row):
    ntok, width = tokens.shape
    cut = width // 8
    return pl.pallas_call(
        route_kernel,
        grid_spec=pltpu.PrefetchScalarGridSpec(
            num_scalar_prefetch=1,
            grid=(1,),
            in_specs=[
                pl.BlockSpec((ntok, cut), lambda i, c: (0, c[0])),
                pl.BlockSpec((ntok, cut), lambda i, c: (0, c[0])),
                whole(ids_t.shape),
                whole(rw_t.shape),
                whole(slot_row.shape),
            ],
            out_specs=[whole((ntok + META, cut)), whole((ntok, cut))],
        ),
        out_shape=[
            jax.ShapeDtypeStruct((ntok + META, cut), BF16),
            jax.ShapeDtypeStruct((ntok, cut), BF16),
        ],
        compiler_params=params(),
        name="route",
    )(col, tokens, cotangent, ids_t, rw_t, slot_row)


def one_hot(place):
    slots, ntok = place.shape
    spread = jnp.broadcast_to(place[:, None, :], (slots, CAP, ntok)).reshape(slots * CAP, ntok)
    at = lax.broadcasted_iota(jnp.int32, (slots * CAP, ntok), 0) % CAP
    return spread == at.astype(F32)


def row_weights(hot, weight):
    slots, ntok = weight.shape
    spread = jnp.broadcast_to(weight[:, None, :], (slots, CAP, ntok)).reshape(slots * CAP, ntok)
    return jnp.sum(jnp.where(hot, spread, 0.0), axis=1, keepdims=True)


def as_bf16(hot):
    return jnp.where(hot, 1.0, 0.0).astype(BF16)


def put_rows(rows, send_ref):
    for l in range(rows.shape[0] // CAP):
        part = rows[l * CAP : (l + 1) * CAP]
        send_ref[2 * l] = part
        send_ref[2 * l + 1] = part


def pick_x_kernel(z_ref, x_ref, send_ref, place_ref, weight_ref):
    ntok = x_ref.shape[1] - META
    left = x_ref[0, ntok : ntok + META, 0:128].astype(F32)
    right = x_ref[0, ntok : ntok + META, 128:256].astype(F32)
    slots = left[0:8]
    w = right[0:8] + left[8:16] + right[8:16]
    first = (z_ref[0] * 16).astype(F32)
    local = lax.broadcasted_iota(jnp.int32, (16, ntok), 0).astype(F32) + first
    chosen = jnp.zeros((16, ntok), F32)
    weight = jnp.zeros((16, ntok), F32)
    for k in range(8):
        same = local == slots[k : k + 1, :]
        chosen = jnp.where(same, 1.0, chosen)
        weight = jnp.where(same, w[k : k + 1, :], weight)
    row = lax.broadcasted_iota(jnp.int32, (ntok, ntok), 0)
    column = lax.broadcasted_iota(jnp.int32, (ntok, ntok), 1)
    earlier = jnp.where(row < column, 1.0, 0.0).astype(BF16)
    before = nn(chosen.astype(BF16), earlier)
    place = jnp.where(chosen > 0.0, before, -1.0)
    place_ref[0] = place
    weight_ref[0] = weight
    rows = nn(as_bf16(one_hot(place)), x_ref[0, 0:ntok, :])
    put_rows(rows.astype(BF16), send_ref)


def pick_x(zs, x_all):
    blocks, rows, cut = x_all.shape
    ntok = rows - META
    return pl.pallas_call(
        pick_x_kernel,
        grid_spec=pltpu.PrefetchScalarGridSpec(
            num_scalar_prefetch=1,
            grid=(blocks,),
            in_specs=[pl.BlockSpec((1, rows, cut), lambda b, z: (b, 0, 0))],
            out_specs=[
                pl.BlockSpec((32, CAP, cut), lambda b, z: (0, b, 0)),
                pl.BlockSpec((1, 16, ntok), lambda b, z: (b, 0, 0)),
                pl.BlockSpec((1, 16, ntok), lambda b, z: (b, 0, 0)),
            ],
        ),
        out_shape=[
            jax.ShapeDtypeStruct((32, blocks * CAP, cut), BF16),
            jax.ShapeDtypeStruct((blocks, 16, ntok), F32),
            jax.ShapeDtypeStruct((blocks, 16, ntok), F32),
        ],
        compiler_params=params(),
        name="pick_x",
    )(zs, x_all)


def pick_g_kernel(g_ref, place_ref, weight_ref, send_ref):
    hot = one_hot(place_ref[0])
    rows = nn(as_bf16(hot), g_ref[0]) * row_weights(hot, weight_ref[0])
    put_rows(rows.astype(BF16), send_ref)


def pick_g(g_all, place, weight):
    blocks, ntok, cut = g_all.shape
    return pl.pallas_call(
        pick_g_kernel,
        grid=(blocks,),
        in_specs=[
            pl.BlockSpec((1, ntok, cut), lambda b: (b, 0, 0)),
            pl.BlockSpec((1, 16, ntok), lambda b: (b, 0, 0)),
            pl.BlockSpec((1, 16, ntok), lambda b: (b, 0, 0)),
        ],
        out_specs=pl.BlockSpec((32, CAP, cut), lambda b: (0, b, 0)),
        out_shape=jax.ShapeDtypeStruct((32, blocks * CAP, cut), BF16),
        compiler_params=params(),
        name="pick_g",
    )(g_all, place, weight)


def chunk(ref, e):
    return jnp.concatenate([ref[q * 8 + e] for q in range(4)], axis=0)


def put_chunk(ref, e, rows):
    for q in range(4):
        ref[q * 8 + e] = rows[q * 128 : (q + 1) * 128]


def forward_kernel(x_ref, wg_ref, wu_ref, wd_ref, out_ref, gate_ref, up_ref, hidden_ref):
    cut = x_ref.shape[2]

    def first(e, _):
        at = pl.ds(pl.multiple_of(e * cut, cut), cut)
        x = chunk(x_ref, e)
        gate_ref[...] += nn(x, wg_ref[0, at, :])
        up_ref[...] += nn(x, wu_ref[0, at, :])
        return 0

    gate_ref[...] = jnp.zeros_like(gate_ref)
    up_ref[...] = jnp.zeros_like(up_ref)
    lax.fori_loop(0, 8, first, 0)
    gate = gate_ref[...]
    hidden_ref[...] = (gate * jax.nn.sigmoid(gate) * up_ref[...]).astype(BF16)

    def second(e, _):
        at = pl.ds(pl.multiple_of(e * cut, cut), cut)
        put_chunk(out_ref, e, nn(hidden_ref[...], wd_ref[0, :, at]).astype(BF16))
        return 0

    lax.fori_loop(0, 8, second, 0)


def forward(x_rows, wg, wu, wd):
    rows, ff = 512, wg.shape[2]
    return pl.pallas_call(
        forward_kernel,
        out_shape=[
            jax.ShapeDtypeStruct(x_rows.shape, BF16),
            jax.ShapeDtypeStruct((rows, ff), F32),
            jax.ShapeDtypeStruct((rows, ff), F32),
            jax.ShapeDtypeStruct((rows, ff), BF16),
        ],
        compiler_params=params(),
        cost_estimate=pl.CostEstimate(
            flops=6 * rows * 2048 * ff, bytes_accessed=11 * 2**20, transcendentals=rows * ff
        ),
        name="forward",
    )(x_rows, wg, wu, wd)


def backward_kernel(
    g_ref, gate_ref, up_ref, wg_ref, wu_ref, wd_ref, in_ref, dgate_ref, dup_ref, back_ref
):
    cut = g_ref.shape[2]

    def first(e, _):
        at = pl.ds(pl.multiple_of(e * cut, cut), cut)
        back_ref[...] += nt(chunk(g_ref, e), wd_ref[0, :, at])
        return 0

    back_ref[...] = jnp.zeros_like(back_ref)
    lax.fori_loop(0, 8, first, 0)
    back, gate = back_ref[...], gate_ref[...]
    sigma = jax.nn.sigmoid(gate)
    dgate_ref[...] = (back * up_ref[...] * sigma * (1.0 + gate * (1.0 - sigma))).astype(BF16)
    dup_ref[...] = (back * (gate * sigma)).astype(BF16)

    def second(e, _):
        at = pl.ds(pl.multiple_of(e * cut, cut), cut)
        piece = nt(dgate_ref[...], wg_ref[0, at, :]) + nt(dup_ref[...], wu_ref[0, at, :])
        put_chunk(in_ref, e, piece.astype(BF16))
        return 0

    lax.fori_loop(0, 8, second, 0)


def backward(g_rows, gate, up, wg, wu, wd):
    rows, ff = gate.shape
    return pl.pallas_call(
        backward_kernel,
        out_shape=[
            jax.ShapeDtypeStruct(g_rows.shape, BF16),
            jax.ShapeDtypeStruct((rows, ff), BF16),
            jax.ShapeDtypeStruct((rows, ff), BF16),
        ],
        scratch_shapes=[pltpu.VMEM((rows, ff), F32)],
        compiler_params=params(),
        cost_estimate=pl.CostEstimate(
            flops=6 * rows * 2048 * ff, bytes_accessed=11 * 2**20, transcendentals=rows * ff
        ),
        name="backward",
    )(g_rows, gate, up, wg, wu, wd)


def grads_kernel(x_ref, g_ref, hidden_ref, dgate_ref, dup_ref, gg_ref, gu_ref, gd_ref):
    cut = x_ref.shape[2]

    def step(e, _):
        at = pl.ds(pl.multiple_of(e * cut, cut), cut)
        x = chunk(x_ref, e)
        gg_ref[0, at, :] = tn(x, dgate_ref[...]).astype(BF16)
        gu_ref[0, at, :] = tn(x, dup_ref[...]).astype(BF16)
        gd_ref[0, :, at] = tn(hidden_ref[...], chunk(g_ref, e)).astype(BF16)
        return 0

    lax.fori_loop(0, 8, step, 0)


def grads(x_rows, g_rows, hidden, dgate, dup):
    rows, ff = hidden.shape
    width = 8 * x_rows.shape[2]
    return pl.pallas_call(
        grads_kernel,
        out_shape=[
            jax.ShapeDtypeStruct((1, width, ff), BF16),
            jax.ShapeDtypeStruct((1, width, ff), BF16),
            jax.ShapeDtypeStruct((1, ff, width), BF16),
        ],
        compiler_params=params(),
        cost_estimate=pl.CostEstimate(
            flops=6 * rows * 2048 * ff, bytes_accessed=10 * 2**20, transcendentals=0
        ),
        name="grads",
    )(x_rows, g_rows, hidden, dgate, dup)


def add_rows(place, scale, back_ref, sum_ref):
    hot = one_hot(place)
    rows = jnp.concatenate(
        [back_ref[2 * l].astype(F32) + back_ref[2 * l + 1].astype(F32) for l in range(16)], axis=0
    )
    if scale is not None:
        rows = rows * row_weights(hot, scale)
    hi = rows.astype(BF16)
    low = (rows - hi.astype(F32)).astype(BF16)
    pick = as_bf16(hot)
    sum_ref[0] = (tn(pick, hi) + tn(pick, low)).astype(BF16)


def join_out_kernel(place_ref, weight_ref, back_ref, sum_ref):
    add_rows(place_ref[0], weight_ref[0], back_ref, sum_ref)


def join_in_kernel(place_ref, back_ref, sum_ref):
    add_rows(place_ref[0], None, back_ref, sum_ref)


def join(kernel, per_block, back, name):
    blocks, _, ntok = per_block[0].shape
    cut = back.shape[2]
    return pl.pallas_call(
        kernel,
        grid=(blocks,),
        in_specs=[pl.BlockSpec((1, 16, ntok), lambda b: (b, 0, 0)) for _ in per_block]
        + [pl.BlockSpec((32, CAP, cut), lambda b: (0, b, 0))],
        out_specs=pl.BlockSpec((1, ntok, cut), lambda b: (b, 0, 0)),
        out_shape=jax.ShapeDtypeStruct((blocks, ntok, cut), BF16),
        compiler_params=params(),
        name=name,
    )(*per_block, back)


def last_kernel(part_ref, out_ref, in_ref):
    cut = part_ref.shape[2]
    for e in range(8):
        total = part_ref[e].astype(F32)
        for z in range(1, 8):
            total = total + part_ref[z * 8 + e].astype(F32)
        half = total.shape[0] // 2
        out_ref[:, e * cut : (e + 1) * cut] = total[:half].astype(BF16)
        in_ref[:, e * cut : (e + 1) * cut] = total[half:].astype(BF16)


def last(parts):
    _, two, cut = parts.shape
    shape = jax.ShapeDtypeStruct((two // 2, 8 * cut), BF16)
    return pl.pallas_call(
        last_kernel, out_shape=[shape, shape], compiler_params=params(), name="last"
    )(parts)


def swap(buffer, axes):
    return lax.all_to_all(buffer, axes, split_axis=0, concat_axis=0, tiled=True)


def on_device(
    tokens, expert_ids, route_weight, expert_slot, gate_weight, up_weight, down_weight, cotangent
):
    col = lax.axis_index(EX).astype(jnp.int32).reshape(1)
    zs = lax.axis_index("z").astype(jnp.int32).reshape(1)
    x_cut, g_cut = route(
        col, tokens, cotangent, expert_ids.T, route_weight.T, expert_slot.reshape(1, -1)
    )
    x_all = lax.all_gather(x_cut, "z", axis=0, tiled=False)
    g_all = lax.all_gather(g_cut, "z", axis=0, tiled=False)
    x_send, place, weight = pick_x(zs, x_all)
    x_rows = swap(x_send, PLANE)
    g_send = pick_g(g_all, place, weight)
    g_rows = swap(g_send, PLANE)
    out_send, gate, up, hidden = forward(x_rows, gate_weight, up_weight, down_weight)
    out_back = swap(out_send, PLANE)
    in_send, dgate, dup = backward(g_rows, gate, up, gate_weight, up_weight, down_weight)
    in_back = swap(in_send, PLANE)
    grad_gate, grad_up, grad_down = grads(x_rows, g_rows, hidden, dgate, dup)
    y_part = join(join_out_kernel, (place, weight), out_back, "join_out")
    dx_part = join(join_in_kernel, (place,), in_back, "join_in")
    cut = y_part.shape[2]
    both = jnp.concatenate(
        [y_part.reshape(64, 16, cut), dx_part.reshape(64, 16, cut)], axis=1
    )
    layer_out, input_grad = last(swap(both, ("z", "xh", "y")))
    return layer_out, input_grad, grad_gate, grad_up, grad_down


def solution(mesh):
    fine = Mesh(mesh.devices.reshape(8, 2, 2, 2, 4), ("z", "xl", "core", "xh", "y"))
    rows, every = P(DP, None), P(DP + EX, None)
    half = P(DP + EX, None, None)
    return jax.shard_map(
        on_device,
        mesh=fine,
        in_specs=(rows, rows, rows, P(), half, half, half, rows),
        out_specs=(every, every, half, half, half),
        check_vma=False,
    )
```

```python
import functools

import jax
import jax.numpy as jnp
from jax import lax
from jax.experimental import pallas as pl
from jax.experimental.pallas import tpu as pltpu
from jax.sharding import Mesh, PartitionSpec as P

DP = ("z", "xl", "core")
EX = ("xh", "y")
PLANE = ("xl", "core", "xh", "y")
BF16 = jnp.bfloat16
F32 = jnp.float32
CAP = 16
META = 16


def nn(a, b):
    return lax.dot_general(a, b, (((1,), (0,)), ((), ())), preferred_element_type=F32)


def nt(a, b):
    return lax.dot_general(a, b, (((1,), (1,)), ((), ())), preferred_element_type=F32)


def tn(a, b):
    return lax.dot_general(a, b, (((0,), (0,)), ((), ())), preferred_element_type=F32)


def params(mib=16):
    return pltpu.CompilerParams(vmem_limit_bytes=mib * 2**20)


def whole(shape):
    return pl.BlockSpec(shape, lambda *_: (0,) * len(shape))


def route_kernel(col_ref, tok_ref, cot_ref, ids_ref, rw_ref, slot_ref, x_ref, g_ref):
    ntok = tok_ref.shape[0]
    g_ref[...] = cot_ref[...]
    table = jnp.broadcast_to(slot_ref[...], (8, slot_ref.shape[1]))
    slots = jnp.take_along_axis(table, ids_ref[...], axis=1, mode="promise_in_bounds").astype(F32)
    w = rw_ref[...]
    hi = w.astype(BF16).astype(F32)
    rest = w - hi
    mid = rest.astype(BF16).astype(F32)
    low = rest - mid
    left = jnp.concatenate([slots, mid], axis=0)
    right = jnp.concatenate([hi, low], axis=0)
    tok, left, right = tok_ref[...], left.astype(BF16), right.astype(BF16)
    for z in range(x_ref.shape[0]):
        x_ref[z, 0:ntok, :] = tok
        x_ref[z, ntok : ntok + META, 0:128] = left
        x_ref[z, ntok : ntok + META, 128:256] = right


def route(col, tokens, cotangent, ids_t, rw_t, slot_row):
    ntok, width = tokens.shape
    cut = width // 8
    return pl.pallas_call(
        route_kernel,
        grid_spec=pltpu.PrefetchScalarGridSpec(
            num_scalar_prefetch=1,
            grid=(1,),
            in_specs=[
                pl.BlockSpec((ntok, cut), lambda i, c: (0, c[0])),
                pl.BlockSpec((ntok, cut), lambda i, c: (0, c[0])),
                whole(ids_t.shape),
                whole(rw_t.shape),
                whole(slot_row.shape),
            ],
            out_specs=[whole((8, ntok + META, cut)), whole((ntok, cut))],
        ),
        out_shape=[
            jax.ShapeDtypeStruct((8, ntok + META, cut), BF16),
            jax.ShapeDtypeStruct((ntok, cut), BF16),
        ],
        compiler_params=params(60),
        name="route",
    )(col, tokens, cotangent, ids_t, rw_t, slot_row)


def one_hot(place):
    slots, ntok = place.shape
    spread = jnp.broadcast_to(place[:, None, :], (slots, CAP, ntok)).reshape(slots * CAP, ntok)
    at = lax.broadcasted_iota(jnp.int32, (slots * CAP, ntok), 0) % CAP
    return spread == at.astype(F32)


def row_weights(hot, weight):
    slots, ntok = weight.shape
    spread = jnp.broadcast_to(weight[:, None, :], (slots, CAP, ntok)).reshape(slots * CAP, ntok)
    return jnp.sum(jnp.where(hot, spread, 0.0), axis=1, keepdims=True)


def as_bf16(hot):
    return jnp.where(hot, 1.0, 0.0).astype(BF16)


def put_rows(rows, send_ref):
    for l in range(rows.shape[0] // CAP):
        part = rows[l * CAP : (l + 1) * CAP]
        send_ref[2 * l] = part
        send_ref[2 * l + 1] = part


def pick_x_kernel(z_ref, x_ref, send_ref, place_ref, weight_ref):
    ntok = x_ref.shape[1] - META
    left = x_ref[0, ntok : ntok + META, 0:128].astype(F32)
    right = x_ref[0, ntok : ntok + META, 128:256].astype(F32)
    slots = left[0:8]
    w = right[0:8] + left[8:16] + right[8:16]
    first = (z_ref[0] * 16).astype(F32)
    local = lax.broadcasted_iota(jnp.int32, (16, ntok), 0).astype(F32) + first
    chosen = jnp.zeros((16, ntok), F32)
    weight = jnp.zeros((16, ntok), F32)
    for k in range(8):
        same = local == slots[k : k + 1, :]
        chosen = jnp.where(same, 1.0, chosen)
        weight = jnp.where(same, w[k : k + 1, :], weight)
    row = lax.broadcasted_iota(jnp.int32, (ntok, ntok), 0)
    column = lax.broadcasted_iota(jnp.int32, (ntok, ntok), 1)
    earlier = jnp.where(row < column, 1.0, 0.0).astype(BF16)
    before = nn(chosen.astype(BF16), earlier)
    place = jnp.where(chosen > 0.0, before, -1.0)
    place_ref[0] = place
    weight_ref[0] = weight
    rows = nn(as_bf16(one_hot(place)), x_ref[0, 0:ntok, :])
    put_rows(rows.astype(BF16), send_ref)


def pick_x(zs, x_all):
    blocks, rows, cut = x_all.shape
    ntok = rows - META
    return pl.pallas_call(
        pick_x_kernel,
        grid_spec=pltpu.PrefetchScalarGridSpec(
            num_scalar_prefetch=1,
            grid=(blocks,),
            in_specs=[pl.BlockSpec((1, rows, cut), lambda b, z: (b, 0, 0))],
            out_specs=[
                pl.BlockSpec((32, CAP, cut), lambda b, z: (0, b, 0)),
                pl.BlockSpec((1, 16, ntok), lambda b, z: (b, 0, 0)),
                pl.BlockSpec((1, 16, ntok), lambda b, z: (b, 0, 0)),
            ],
        ),
        out_shape=[
            jax.ShapeDtypeStruct((32, blocks * CAP, cut), BF16),
            jax.ShapeDtypeStruct((blocks, 16, ntok), F32),
            jax.ShapeDtypeStruct((blocks, 16, ntok), F32),
        ],
        compiler_params=params(),
        name="pick_x",
    )(zs, x_all)


def pick_g_kernel(z_ref, *refs):
    g_refs, (place_ref, weight_ref, send_ref) = refs[:8], refs[8:]
    for shift, g_ref in enumerate(g_refs):
        block = lax.rem(z_ref[0] + 8 - shift, 8)
        hot = one_hot(place_ref[block])
        rows = nn(as_bf16(hot), g_ref[...]) * row_weights(hot, weight_ref[block])
        put_rows(rows.astype(BF16), send_ref.at[:, pl.ds(pl.multiple_of(block * CAP, CAP), CAP), :])


def pick_g(zs, g_blocks, place, weight):
    blocks = place.shape[0]
    ntok, cut = g_blocks[0].shape
    return pl.pallas_call(
        pick_g_kernel,
        grid_spec=pltpu.PrefetchScalarGridSpec(
            num_scalar_prefetch=1,
            grid=(1,),
            in_specs=[whole((ntok, cut))] * 8 + [whole(place.shape), whole(weight.shape)],
            out_specs=whole((32, blocks * CAP, cut)),
        ),
        out_shape=jax.ShapeDtypeStruct((32, blocks * CAP, cut), BF16),
        compiler_params=params(),
        name="pick_g",
    )(zs, *g_blocks, place, weight)


def chunk(ref, e):
    return jnp.concatenate([ref[q * 8 + e] for q in range(4)], axis=0)


def put_chunk(ref, e, rows):
    for q in range(4):
        ref[q * 8 + e] = rows[q * 128 : (q + 1) * 128]


def forward_kernel(x_ref, wg_ref, wu_ref, wd_ref, out_ref, gate_ref, up_ref, hidden_ref):
    cut = x_ref.shape[2]

    def first(e, _):
        at = pl.ds(pl.multiple_of(e * cut, cut), cut)
        x = chunk(x_ref, e)
        gate_ref[...] += nn(x, wg_ref[0, at, :])
        up_ref[...] += nn(x, wu_ref[0, at, :])
        return 0

    gate_ref[...] = jnp.zeros_like(gate_ref)
    up_ref[...] = jnp.zeros_like(up_ref)
    lax.fori_loop(0, 8, first, 0)
    gate = gate_ref[...]
    hidden_ref[...] = (gate * jax.nn.sigmoid(gate) * up_ref[...]).astype(BF16)

    def second(e, _):
        at = pl.ds(pl.multiple_of(e * cut, cut), cut)
        put_chunk(out_ref, e, nn(hidden_ref[...], wd_ref[0, :, at]).astype(BF16))
        return 0

    lax.fori_loop(0, 8, second, 0)


def forward(x_rows, wg, wu, wd):
    rows, ff = 512, wg.shape[2]
    return pl.pallas_call(
        forward_kernel,
        out_shape=[
            jax.ShapeDtypeStruct(x_rows.shape, BF16),
            jax.ShapeDtypeStruct((rows, ff), F32),
            jax.ShapeDtypeStruct((rows, ff), F32),
            jax.ShapeDtypeStruct((rows, ff), BF16),
        ],
        compiler_params=params(),
        cost_estimate=pl.CostEstimate(
            flops=6 * rows * 2048 * ff, bytes_accessed=11 * 2**20, transcendentals=rows * ff
        ),
        name="forward",
    )(x_rows, wg, wu, wd)


def backward_kernel(
    g_ref, gate_ref, up_ref, wg_ref, wu_ref, wd_ref, in_ref, dgate_ref, dup_ref, back_ref
):
    cut = g_ref.shape[2]

    def first(e, _):
        at = pl.ds(pl.multiple_of(e * cut, cut), cut)
        back_ref[...] += nt(chunk(g_ref, e), wd_ref[0, :, at])
        return 0

    back_ref[...] = jnp.zeros_like(back_ref)
    lax.fori_loop(0, 8, first, 0)
    back, gate = back_ref[...], gate_ref[...]
    sigma = jax.nn.sigmoid(gate)
    dgate_ref[...] = (back * up_ref[...] * sigma * (1.0 + gate * (1.0 - sigma))).astype(BF16)
    dup_ref[...] = (back * (gate * sigma)).astype(BF16)

    def second(e, _):
        at = pl.ds(pl.multiple_of(e * cut, cut), cut)
        piece = nt(dgate_ref[...], wg_ref[0, at, :]) + nt(dup_ref[...], wu_ref[0, at, :])
        put_chunk(in_ref, e, piece.astype(BF16))
        return 0

    lax.fori_loop(0, 8, second, 0)


def backward(g_rows, gate, up, wg, wu, wd):
    rows, ff = gate.shape
    return pl.pallas_call(
        backward_kernel,
        out_shape=[
            jax.ShapeDtypeStruct(g_rows.shape, BF16),
            jax.ShapeDtypeStruct((rows, ff), BF16),
            jax.ShapeDtypeStruct((rows, ff), BF16),
        ],
        scratch_shapes=[pltpu.VMEM((rows, ff), F32)],
        compiler_params=params(),
        cost_estimate=pl.CostEstimate(
            flops=6 * rows * 2048 * ff, bytes_accessed=11 * 2**20, transcendentals=rows * ff
        ),
        name="backward",
    )(g_rows, gate, up, wg, wu, wd)


def grads_kernel(x_ref, g_ref, hidden_ref, dgate_ref, dup_ref, gg_ref, gu_ref, gd_ref):
    cut = x_ref.shape[2]

    def step(e, _):
        at = pl.ds(pl.multiple_of(e * cut, cut), cut)
        x = chunk(x_ref, e)
        gg_ref[0, at, :] = tn(x, dgate_ref[...]).astype(BF16)
        gu_ref[0, at, :] = tn(x, dup_ref[...]).astype(BF16)
        gd_ref[0, :, at] = tn(hidden_ref[...], chunk(g_ref, e)).astype(BF16)
        return 0

    lax.fori_loop(0, 8, step, 0)


def grads(x_rows, g_rows, hidden, dgate, dup):
    rows, ff = hidden.shape
    width = 8 * x_rows.shape[2]
    return pl.pallas_call(
        grads_kernel,
        out_shape=[
            jax.ShapeDtypeStruct((1, width, ff), BF16),
            jax.ShapeDtypeStruct((1, width, ff), BF16),
            jax.ShapeDtypeStruct((1, ff, width), BF16),
        ],
        compiler_params=params(),
        cost_estimate=pl.CostEstimate(
            flops=6 * rows * 2048 * ff, bytes_accessed=10 * 2**20, transcendentals=0
        ),
        name="grads",
    )(x_rows, g_rows, hidden, dgate, dup)


def add_rows(place, scale, back, like):
    hot = one_hot(place)
    rows = jnp.concatenate(
        [back[2 * l].astype(F32) + back[2 * l + 1].astype(F32) for l in range(16)], axis=0
    )
    if scale is not None:
        rows = rows * row_weights(hot, scale)
    hi = rows.astype(BF16)
    low = (rows - hi.astype(F32)).astype(BF16)
    pick = as_bf16(hot)
    return (tn(pick, hi) + tn(pick, low)).astype(BF16).reshape(like)


def join_kernel(weighted, *refs):
    place_ref, back_ref, sum_ref = refs[0], refs[2 if weighted else 1], refs[-1]
    blocks = place_ref.shape[0]
    eighth, part, cut = sum_ref.shape[0] // blocks, sum_ref.shape[1], sum_ref.shape[2]

    def step(b, _):
        rows = pl.ds(pl.multiple_of(b * CAP, CAP), CAP)
        scale = refs[1][b] if weighted else None
        total = add_rows(place_ref[b], scale, back_ref.at[:, rows, :], (eighth, part, cut))
        sum_ref[pl.ds(b * eighth, eighth)] = total
        return 0

    lax.fori_loop(0, blocks, step, 0)


def join(per_block, back, half, buffer, name):
    blocks, _, ntok = per_block[0].shape
    cut = back.shape[2]
    part = ntok // 8
    given = [] if buffer is None else [buffer]
    count = len(per_block) + 1
    return pl.pallas_call(
        functools.partial(join_kernel, len(per_block) == 2),
        grid=(1,),
        in_specs=[whole(a.shape) for a in per_block]
        + [whole(back.shape)]
        + [pl.BlockSpec(memory_space=pl.ANY) for _ in given],
        out_specs=pl.BlockSpec((8 * blocks, part, cut), lambda i: (0, half, 0)),
        out_shape=jax.ShapeDtypeStruct((8 * blocks, 2 * part, cut), BF16),
        input_output_aliases={count: 0} if given else {},
        compiler_params=params(),
        name=name,
    )(*per_block, back, *given)


def last_kernel(part_ref, out_ref, in_ref):
    cut = part_ref.shape[2]
    for e in range(8):
        total = part_ref[e].astype(F32)
        for z in range(1, 8):
            total = total + part_ref[z * 8 + e].astype(F32)
        half = total.shape[0] // 2
        out_ref[:, e * cut : (e + 1) * cut] = total[:half].astype(BF16)
        in_ref[:, e * cut : (e + 1) * cut] = total[half:].astype(BF16)


def last(parts):
    _, two, cut = parts.shape
    shape = jax.ShapeDtypeStruct((two // 2, 8 * cut), BF16)
    return pl.pallas_call(
        last_kernel, out_shape=[shape, shape], compiler_params=params(), name="last"
    )(parts)


def swap(buffer, axes):
    return lax.all_to_all(buffer, axes, split_axis=0, concat_axis=0, tiled=True)


def on_device(
    tokens, expert_ids, route_weight, expert_slot, gate_weight, up_weight, down_weight, cotangent
):
    col = lax.axis_index(EX).astype(jnp.int32).reshape(1)
    zs = lax.axis_index("z").astype(jnp.int32).reshape(1)
    x_cut, g_cut = route(
        col, tokens, cotangent, expert_ids.T, route_weight.T, expert_slot.reshape(1, -1)
    )
    x_all = swap(x_cut, ("z",))
    x_send, place, weight = pick_x(zs, x_all)
    g_blocks = [g_cut] + [
        lax.ppermute(g_cut, "z", [(z, (z + shift) % 8) for z in range(8)]) for shift in range(1, 8)
    ]
    x_rows = swap(x_send, PLANE)
    g_send = pick_g(zs, g_blocks, place, weight)
    g_rows = swap(g_send, PLANE)
    out_send, gate, up, hidden = forward(x_rows, gate_weight, up_weight, down_weight)
    out_back = swap(out_send, PLANE)
    in_send, dgate, dup = backward(g_rows, gate, up, gate_weight, up_weight, down_weight)
    in_back = swap(in_send, PLANE)
    weight_grads = grads(x_rows, g_rows, hidden, dgate, dup)
    both = join((place, weight), out_back, 0, None, "join_out")
    in_back, both, weight_grads = lax.optimization_barrier((in_back, both, weight_grads))
    both = join((place,), in_back, 1, both, "join_in")
    layer_out, input_grad = last(swap(both, ("z", "xh", "y")))
    return layer_out, input_grad, *weight_grads


def solution(mesh):
    fine = Mesh(mesh.devices.reshape(8, 2, 2, 2, 4), ("z", "xl", "core", "xh", "y"))
    rows, every = P(DP, None), P(DP + EX, None)
    half = P(DP + EX, None, None)
    return jax.shard_map(
        on_device,
        mesh=fine,
        in_specs=(rows, rows, rows, P(), half, half, half, rows),
        out_specs=(every, every, half, half, half),
        check_vma=False,
    )
```

```python
import jax
import jax.numpy as jnp
from jax import lax
from jax.experimental import pallas as pl
from jax.experimental.pallas import tpu as pltpu
from jax.sharding import Mesh, PartitionSpec as P

DP = ("z", "xl", "core")
EX = ("xh", "y")
PLANE = ("xl", "core", "xh", "y")
BF16 = jnp.bfloat16
F32 = jnp.float32
CAP = 16
META = 16


def nn(a, b):
    return lax.dot_general(a, b, (((1,), (0,)), ((), ())), preferred_element_type=F32)


def nt(a, b):
    return lax.dot_general(a, b, (((1,), (1,)), ((), ())), preferred_element_type=F32)


def tn(a, b):
    return lax.dot_general(a, b, (((0,), (0,)), ((), ())), preferred_element_type=F32)


def params(mib=16):
    return pltpu.CompilerParams(vmem_limit_bytes=mib * 2**20)


def whole(shape):
    return pl.BlockSpec(shape, lambda *_: (0,) * len(shape))


def route_kernel(col_ref, tok_ref, cot_ref, ids_ref, rw_ref, slot_ref, x_ref, g_ref):
    ntok = tok_ref.shape[0]
    g_ref[...] = cot_ref[...]
    table = jnp.broadcast_to(slot_ref[...], (8, slot_ref.shape[1]))
    slots = jnp.take_along_axis(table, ids_ref[...], axis=1, mode="promise_in_bounds").astype(F32)
    w = rw_ref[...]
    hi = w.astype(BF16).astype(F32)
    rest = w - hi
    mid = rest.astype(BF16).astype(F32)
    low = rest - mid
    left = jnp.concatenate([slots, mid], axis=0)
    right = jnp.concatenate([hi, low], axis=0)
    tok, left, right = tok_ref[...], left.astype(BF16), right.astype(BF16)
    for z in range(x_ref.shape[0]):
        x_ref[z, 0:ntok, :] = tok
        x_ref[z, ntok : ntok + META, 0:128] = left
        x_ref[z, ntok : ntok + META, 128:256] = right


def route(col, tokens, cotangent, ids_t, rw_t, slot_row):
    ntok, width = tokens.shape
    cut = width // 8
    return pl.pallas_call(
        route_kernel,
        grid_spec=pltpu.PrefetchScalarGridSpec(
            num_scalar_prefetch=1,
            grid=(1,),
            in_specs=[
                pl.BlockSpec((ntok, cut), lambda i, c: (0, c[0])),
                pl.BlockSpec((ntok, cut), lambda i, c: (0, c[0])),
                whole(ids_t.shape),
                whole(rw_t.shape),
                whole(slot_row.shape),
            ],
            out_specs=[whole((8, ntok + META, cut)), whole((ntok, cut))],
        ),
        out_shape=[
            jax.ShapeDtypeStruct((8, ntok + META, cut), BF16),
            jax.ShapeDtypeStruct((ntok, cut), BF16),
        ],
        compiler_params=params(60),
        name="route",
    )(col, tokens, cotangent, ids_t, rw_t, slot_row)


def one_hot(place):
    slots, ntok = place.shape
    spread = jnp.broadcast_to(place[:, None, :], (slots, CAP, ntok)).reshape(slots * CAP, ntok)
    at = lax.broadcasted_iota(jnp.int32, (slots * CAP, ntok), 0) % CAP
    return spread == at.astype(F32)


def row_weights(hot, weight):
    slots, ntok = weight.shape
    spread = jnp.broadcast_to(weight[:, None, :], (slots, CAP, ntok)).reshape(slots * CAP, ntok)
    return jnp.sum(jnp.where(hot, spread, 0.0), axis=1, keepdims=True)


def as_bf16(hot):
    return jnp.where(hot, 1.0, 0.0).astype(BF16)


def put_rows(rows, send_ref):
    for l in range(rows.shape[0] // CAP):
        part = rows[l * CAP : (l + 1) * CAP]
        send_ref[2 * l] = part
        send_ref[2 * l + 1] = part


def pick_x_kernel(z_ref, x_ref, send_ref, place_ref, weight_ref):
    ntok = x_ref.shape[1] - META
    first = (z_ref[0] * 16).astype(F32)
    local = lax.broadcasted_iota(jnp.int32, (16, ntok), 0).astype(F32) + first
    row = lax.broadcasted_iota(jnp.int32, (ntok, ntok), 0)
    column = lax.broadcasted_iota(jnp.int32, (ntok, ntok), 1)
    earlier = jnp.where(row < column, 1.0, 0.0).astype(BF16)
    for b in range(x_ref.shape[0]):
        left = x_ref[b, ntok : ntok + META, 0:128].astype(F32)
        right = x_ref[b, ntok : ntok + META, 128:256].astype(F32)
        slots = left[0:8]
        w = right[0:8] + left[8:16] + right[8:16]
        chosen = jnp.zeros((16, ntok), F32)
        weight = jnp.zeros((16, ntok), F32)
        for k in range(8):
            same = local == slots[k : k + 1, :]
            chosen = jnp.where(same, 1.0, chosen)
            weight = jnp.where(same, w[k : k + 1, :], weight)
        before = nn(chosen.astype(BF16), earlier)
        place = jnp.where(chosen > 0.0, before, -1.0)
        place_ref[b] = place
        weight_ref[b] = weight
        rows = nn(as_bf16(one_hot(place)), x_ref[b, 0:ntok, :])
        put_rows(rows.astype(BF16), send_ref.at[:, b * CAP : (b + 1) * CAP, :])


def pick_x(zs, x_all):
    blocks, rows, cut = x_all.shape
    ntok = rows - META
    return pl.pallas_call(
        pick_x_kernel,
        grid_spec=pltpu.PrefetchScalarGridSpec(
            num_scalar_prefetch=1,
            grid=(1,),
            in_specs=[whole(x_all.shape)],
            out_specs=[
                whole((32, blocks * CAP, cut)),
                whole((blocks, 16, ntok)),
                whole((blocks, 16, ntok)),
            ],
        ),
        out_shape=[
            pltpu.HBM((32, blocks * CAP, cut), BF16),
            jax.ShapeDtypeStruct((blocks, 16, ntok), F32),
            jax.ShapeDtypeStruct((blocks, 16, ntok), F32),
        ],
        compiler_params=params(),
        name="pick_x",
    )(zs, x_all)


def pick_g_kernel(z_ref, *refs):
    g_refs, (place_ref, weight_ref, send_ref) = refs[:8], refs[8:]
    for shift, g_ref in enumerate(g_refs):
        block = lax.rem(z_ref[0] + 8 - shift, 8)
        hot = one_hot(place_ref[block])
        rows = nn(as_bf16(hot), g_ref[...]) * row_weights(hot, weight_ref[block])
        put_rows(rows.astype(BF16), send_ref.at[:, pl.ds(pl.multiple_of(block * CAP, CAP), CAP), :])


def pick_g(zs, g_blocks, place, weight):
    blocks = place.shape[0]
    ntok, cut = g_blocks[0].shape
    return pl.pallas_call(
        pick_g_kernel,
        grid_spec=pltpu.PrefetchScalarGridSpec(
            num_scalar_prefetch=1,
            grid=(1,),
            in_specs=[whole((ntok, cut))] * 8 + [whole(place.shape), whole(weight.shape)],
            out_specs=whole((32, blocks * CAP, cut)),
        ),
        out_shape=jax.ShapeDtypeStruct((32, blocks * CAP, cut), BF16),
        compiler_params=params(),
        name="pick_g",
    )(zs, *g_blocks, place, weight)


def chunk(ref, e):
    return jnp.concatenate([ref[q * 8 + e] for q in range(4)], axis=0)


def put_chunk(ref, e, rows):
    for q in range(4):
        ref[q * 8 + e] = rows[q * 128 : (q + 1) * 128]


def forward_kernel(x_ref, wg_ref, wu_ref, wd_ref, out_ref, gate_ref, up_ref, hidden_ref):
    cut = x_ref.shape[2]

    def first(e, _):
        at = pl.ds(pl.multiple_of(e * cut, cut), cut)
        x = chunk(x_ref, e)
        gate_ref[...] += nn(x, wg_ref[0, at, :])
        up_ref[...] += nn(x, wu_ref[0, at, :])
        return 0

    gate_ref[...] = jnp.zeros_like(gate_ref)
    up_ref[...] = jnp.zeros_like(up_ref)
    lax.fori_loop(0, 8, first, 0)
    gate = gate_ref[...]
    hidden_ref[...] = (gate * jax.nn.sigmoid(gate) * up_ref[...]).astype(BF16)

    def second(e, _):
        at = pl.ds(pl.multiple_of(e * cut, cut), cut)
        put_chunk(out_ref, e, nn(hidden_ref[...], wd_ref[0, :, at]).astype(BF16))
        return 0

    lax.fori_loop(0, 8, second, 0)


def forward(x_rows, wg, wu, wd):
    rows, ff = 512, wg.shape[2]
    return pl.pallas_call(
        forward_kernel,
        out_shape=[
            jax.ShapeDtypeStruct(x_rows.shape, BF16),
            jax.ShapeDtypeStruct((rows, ff), F32),
            jax.ShapeDtypeStruct((rows, ff), F32),
            jax.ShapeDtypeStruct((rows, ff), BF16),
        ],
        compiler_params=params(),
        cost_estimate=pl.CostEstimate(
            flops=6 * rows * 2048 * ff, bytes_accessed=11 * 2**20, transcendentals=rows * ff
        ),
        name="forward",
    )(x_rows, wg, wu, wd)


def backward_kernel(
    g_ref, gate_ref, up_ref, wg_ref, wu_ref, wd_ref, in_ref, dgate_ref, dup_ref, back_ref
):
    cut = g_ref.shape[2]

    def first(e, _):
        at = pl.ds(pl.multiple_of(e * cut, cut), cut)
        back_ref[...] += nt(chunk(g_ref, e), wd_ref[0, :, at])
        return 0

    back_ref[...] = jnp.zeros_like(back_ref)
    lax.fori_loop(0, 8, first, 0)
    back, gate = back_ref[...], gate_ref[...]
    sigma = jax.nn.sigmoid(gate)
    dgate_ref[...] = (back * up_ref[...] * sigma * (1.0 + gate * (1.0 - sigma))).astype(BF16)
    dup_ref[...] = (back * (gate * sigma)).astype(BF16)

    def second(e, _):
        at = pl.ds(pl.multiple_of(e * cut, cut), cut)
        piece = nt(dgate_ref[...], wg_ref[0, at, :]) + nt(dup_ref[...], wu_ref[0, at, :])
        put_chunk(in_ref, e, piece.astype(BF16))
        return 0

    lax.fori_loop(0, 8, second, 0)


def backward(g_rows, gate, up, wg, wu, wd):
    rows, ff = gate.shape
    return pl.pallas_call(
        backward_kernel,
        out_shape=[
            jax.ShapeDtypeStruct(g_rows.shape, BF16),
            jax.ShapeDtypeStruct((rows, ff), BF16),
            jax.ShapeDtypeStruct((rows, ff), BF16),
        ],
        scratch_shapes=[pltpu.VMEM((rows, ff), F32)],
        compiler_params=params(),
        cost_estimate=pl.CostEstimate(
            flops=6 * rows * 2048 * ff, bytes_accessed=11 * 2**20, transcendentals=rows * ff
        ),
        name="backward",
    )(g_rows, gate, up, wg, wu, wd)


def grads_kernel(x_ref, g_ref, hidden_ref, dgate_ref, dup_ref, gg_ref, gu_ref, gd_ref):
    cut = x_ref.shape[2]

    def step(e, _):
        at = pl.ds(pl.multiple_of(e * cut, cut), cut)
        x = chunk(x_ref, e)
        gg_ref[0, at, :] = tn(x, dgate_ref[...]).astype(BF16)
        gu_ref[0, at, :] = tn(x, dup_ref[...]).astype(BF16)
        gd_ref[0, :, at] = tn(hidden_ref[...], chunk(g_ref, e)).astype(BF16)
        return 0

    lax.fori_loop(0, 8, step, 0)


def grads(x_rows, g_rows, hidden, dgate, dup):
    rows, ff = hidden.shape
    width = 8 * x_rows.shape[2]
    return pl.pallas_call(
        grads_kernel,
        out_shape=[
            jax.ShapeDtypeStruct((1, width, ff), BF16),
            jax.ShapeDtypeStruct((1, width, ff), BF16),
            jax.ShapeDtypeStruct((1, ff, width), BF16),
        ],
        compiler_params=params(),
        cost_estimate=pl.CostEstimate(
            flops=6 * rows * 2048 * ff, bytes_accessed=10 * 2**20, transcendentals=0
        ),
        name="grads",
    )(x_rows, g_rows, hidden, dgate, dup)


def add_rows(place, scale, back):
    hot = one_hot(place)
    rows = jnp.concatenate(
        [back[2 * l].astype(F32) + back[2 * l + 1].astype(F32) for l in range(16)], axis=0
    )
    if scale is not None:
        rows = rows * row_weights(hot, scale)
    hi = rows.astype(BF16)
    low = (rows - hi.astype(F32)).astype(BF16)
    pick = as_bf16(hot)
    return tn(pick, hi) + tn(pick, low)


def join_out_kernel(z_ref, place_ref, weight_ref, back_ref, own_ref, *sum_refs):
    for shift, sum_ref in enumerate((own_ref, *sum_refs)):
        block = lax.rem(z_ref[0] + shift, 8)
        rows = back_ref.at[:, pl.ds(pl.multiple_of(block * CAP, CAP), CAP), :]
        sum_ref[...] = add_rows(place_ref[block], weight_ref[block], rows).astype(sum_ref.dtype)


def join_out(zs, place, weight, back):
    ntok, cut = place.shape[2], back.shape[2]
    shapes = [jax.ShapeDtypeStruct((ntok, cut), F32 if s == 0 else BF16) for s in range(8)]
    return pl.pallas_call(
        join_out_kernel,
        grid_spec=pltpu.PrefetchScalarGridSpec(
            num_scalar_prefetch=1,
            grid=(1,),
            in_specs=[whole(place.shape), whole(weight.shape), whole(back.shape)],
            out_specs=[whole((ntok, cut))] * 8,
        ),
        out_shape=shapes,
        compiler_params=params(),
        name="join_out",
    )(zs, place, weight, back)


def join_in_kernel(place_ref, back_ref, sum_ref):
    eighth = sum_ref.shape[0] // place_ref.shape[0]
    for b in range(place_ref.shape[0]):
        total = add_rows(place_ref[b], None, back_ref.at[:, b * CAP : (b + 1) * CAP, :])
        sum_ref[b * eighth : (b + 1) * eighth] = total.astype(BF16).reshape(eighth, *sum_ref.shape[1:])


def join_in(place, back):
    blocks, _, ntok = place.shape
    return pl.pallas_call(
        join_in_kernel,
        out_shape=jax.ShapeDtypeStruct((blocks * 8, ntok // 8, back.shape[2]), BF16),
        compiler_params=params(),
        name="join_in",
    )(place, back)


def total_kernel(col_ref, *refs):
    parts, pieces, total_ref = refs[:8], refs[8:16], refs[16]
    total = parts[0][...]
    for part in parts[1:]:
        total = total + part[...].astype(F32)
    total_ref[...] = total
    count = pieces[0].shape[0]
    for shift, piece in enumerate(pieces):
        to = lax.rem(col_ref[0] + shift, 8)
        piece[...] = total_ref[pl.ds(pl.multiple_of(to * count, count), count), :].astype(BF16)


def total(col, parts):
    ntok, cut = parts[0].shape
    return pl.pallas_call(
        total_kernel,
        grid_spec=pltpu.PrefetchScalarGridSpec(
            num_scalar_prefetch=1,
            grid=(1,),
            in_specs=[whole((ntok, cut))] * 8,
            out_specs=[whole((ntok // 8, cut))] * 8,
            scratch_shapes=[pltpu.VMEM((ntok, cut), F32)],
        ),
        out_shape=[jax.ShapeDtypeStruct((ntok // 8, cut), BF16)] * 8,
        compiler_params=params(),
        name="total",
    )(col, *parts)


def last_kernel(col_ref, *refs):
    pieces, part_ref, out_ref, in_ref = refs[:8], refs[8], refs[9], refs[10]
    cut = part_ref.shape[2]
    for shift, piece in enumerate(pieces):
        at = lax.rem(col_ref[0] + 8 - shift, 8) * cut
        out_ref[:, pl.ds(pl.multiple_of(at, cut), cut)] = piece[...]
    for e in range(8):
        whole_sum = part_ref[e].astype(F32)
        for z in range(1, 8):
            whole_sum = whole_sum + part_ref[z * 8 + e].astype(F32)
        in_ref[:, e * cut : (e + 1) * cut] = whole_sum.astype(BF16)


def last(col, pieces, parts):
    _, count, cut = parts.shape
    shape = jax.ShapeDtypeStruct((count, 8 * cut), BF16)
    return pl.pallas_call(
        last_kernel,
        grid_spec=pltpu.PrefetchScalarGridSpec(
            num_scalar_prefetch=1,
            grid=(1,),
            in_specs=[whole((count, cut))] * 8 + [whole(parts.shape)],
            out_specs=[whole(shape.shape)] * 2,
        ),
        out_shape=[shape, shape],
        compiler_params=params(),
        name="last",
    )(col, *pieces, parts)


def swap(buffer, axes):
    return lax.all_to_all(buffer, axes, split_axis=0, concat_axis=0, tiled=True)


def spread(arrays, axes):
    return [arrays[0]] + [
        lax.ppermute(arrays[shift], axes, [(i, (i + shift) % 8) for i in range(8)])
        for shift in range(1, 8)
    ]


def on_device(
    tokens, expert_ids, route_weight, expert_slot, gate_weight, up_weight, down_weight, cotangent
):
    col = lax.axis_index(EX).astype(jnp.int32).reshape(1)
    zs = lax.axis_index("z").astype(jnp.int32).reshape(1)
    x_cut, g_cut = route(
        col, tokens, cotangent, expert_ids.T, route_weight.T, expert_slot.reshape(1, -1)
    )
    x_all = swap(x_cut, ("z",))
    x_send, place, weight = pick_x(zs, x_all)
    g_blocks = spread([g_cut] * 8, ("z",))
    x_rows = swap(x_send, PLANE)
    g_send = pick_g(zs, g_blocks, place, weight)
    g_rows = swap(g_send, PLANE)
    out_send, gate, up, hidden = forward(x_rows, gate_weight, up_weight, down_weight)
    out_back = pltpu.with_memory_space_constraint(swap(out_send, PLANE), pltpu.HBM)
    in_send, dgate, dup = backward(g_rows, gate, up, gate_weight, up_weight, down_weight)
    weight_grads = grads(x_rows, g_rows, hidden, dgate, dup)
    in_send, weight_grads = lax.optimization_barrier((in_send, weight_grads))
    in_back = swap(in_send, PLANE)
    y_parts = spread(join_out(zs, place, weight, out_back), ("z",))
    pieces = total(col, y_parts)
    in_back, pieces = lax.optimization_barrier((in_back, pieces))
    dx_part = join_in(place, in_back)
    pieces = spread(pieces, EX)
    layer_out, input_grad = last(col, pieces, swap(dx_part, ("z", "xh", "y")))
    return layer_out, input_grad, *weight_grads


def solution(mesh):
    fine = Mesh(mesh.devices.reshape(8, 2, 2, 2, 4), ("z", "xl", "core", "xh", "y"))
    rows, every = P(DP, None), P(DP + EX, None)
    half = P(DP + EX, None, None)
    return jax.shard_map(
        on_device,
        mesh=fine,
        in_specs=(rows, rows, rows, P(), half, half, half, rows),
        out_specs=(every, every, half, half, half),
        check_vma=False,
    )
```

```python
import jax
import jax.numpy as jnp
from jax import lax
from jax.experimental import pallas as pl
from jax.experimental.pallas import tpu as pltpu
from jax.sharding import Mesh, PartitionSpec as P

DP = ("z", "xl", "core")
EX = ("xh", "y")
PLANE = ("xl", "core", "xh", "y")
BF16 = jnp.bfloat16
F32 = jnp.float32
CAP = 16
META = 16


def nn(a, b):
    return lax.dot_general(a, b, (((1,), (0,)), ((), ())), preferred_element_type=F32)


def nt(a, b):
    return lax.dot_general(a, b, (((1,), (1,)), ((), ())), preferred_element_type=F32)


def tn(a, b):
    return lax.dot_general(a, b, (((0,), (0,)), ((), ())), preferred_element_type=F32)


def params(mib=16):
    return pltpu.CompilerParams(vmem_limit_bytes=mib * 2**20)


def whole(shape):
    return pl.BlockSpec(shape, lambda *_: (0,) * len(shape))


def route_kernel(col_ref, tok_ref, cot_ref, ids_ref, rw_ref, slot_ref, x_ref, g_ref):
    ntok = tok_ref.shape[0]
    g_ref[...] = cot_ref[...]
    table = jnp.broadcast_to(slot_ref[...], (8, slot_ref.shape[1]))
    slots = jnp.take_along_axis(table, ids_ref[...], axis=1, mode="promise_in_bounds").astype(F32)
    w = rw_ref[...]
    hi = w.astype(BF16).astype(F32)
    rest = w - hi
    mid = rest.astype(BF16).astype(F32)
    low = rest - mid
    left = jnp.concatenate([slots, mid], axis=0)
    right = jnp.concatenate([hi, low], axis=0)
    tok, left, right = tok_ref[...], left.astype(BF16), right.astype(BF16)
    for z in range(x_ref.shape[0]):
        x_ref[z, 0:ntok, :] = tok
        x_ref[z, ntok : ntok + META, 0:128] = left
        x_ref[z, ntok : ntok + META, 128:256] = right


def route(col, tokens, cotangent, ids_t, rw_t, slot_row):
    ntok, width = tokens.shape
    cut = width // 8
    return pl.pallas_call(
        route_kernel,
        grid_spec=pltpu.PrefetchScalarGridSpec(
            num_scalar_prefetch=1,
            grid=(1,),
            in_specs=[
                pl.BlockSpec((ntok, cut), lambda i, c: (0, c[0])),
                pl.BlockSpec((ntok, cut), lambda i, c: (0, c[0])),
                whole(ids_t.shape),
                whole(rw_t.shape),
                whole(slot_row.shape),
            ],
            out_specs=[whole((8, ntok + META, cut)), whole((ntok, cut))],
        ),
        out_shape=[
            jax.ShapeDtypeStruct((8, ntok + META, cut), BF16),
            jax.ShapeDtypeStruct((ntok, cut), BF16),
        ],
        compiler_params=params(60),
        name="route",
    )(col, tokens, cotangent, ids_t, rw_t, slot_row)


def one_hot(place):
    slots, ntok = place.shape
    spread = jnp.broadcast_to(place[:, None, :], (slots, CAP, ntok)).reshape(slots * CAP, ntok)
    at = lax.broadcasted_iota(jnp.int32, (slots * CAP, ntok), 0) % CAP
    return spread == at.astype(F32)


def row_weights(hot, weight):
    slots, ntok = weight.shape
    spread = jnp.broadcast_to(weight[:, None, :], (slots, CAP, ntok)).reshape(slots * CAP, ntok)
    return jnp.sum(jnp.where(hot, spread, 0.0), axis=1, keepdims=True)


def as_bf16(hot):
    return jnp.where(hot, 1.0, 0.0).astype(BF16)


def put_rows(rows, send_ref):
    for l in range(rows.shape[0] // CAP):
        part = rows[l * CAP : (l + 1) * CAP]
        send_ref[2 * l] = part
        send_ref[2 * l + 1] = part


def pick_x_kernel(z_ref, x_ref, send_ref, place_ref, weight_ref):
    ntok = x_ref.shape[1] - META
    first = (z_ref[0] * 16).astype(F32)
    local = lax.broadcasted_iota(jnp.int32, (16, ntok), 0).astype(F32) + first
    row = lax.broadcasted_iota(jnp.int32, (ntok, ntok), 0)
    column = lax.broadcasted_iota(jnp.int32, (ntok, ntok), 1)
    earlier = jnp.where(row < column, 1.0, 0.0).astype(BF16)
    for b in range(x_ref.shape[0]):
        left = x_ref[b, ntok : ntok + META, 0:128].astype(F32)
        right = x_ref[b, ntok : ntok + META, 128:256].astype(F32)
        slots = left[0:8]
        w = right[0:8] + left[8:16] + right[8:16]
        chosen = jnp.zeros((16, ntok), F32)
        weight = jnp.zeros((16, ntok), F32)
        for k in range(8):
            same = local == slots[k : k + 1, :]
            chosen = jnp.where(same, 1.0, chosen)
            weight = jnp.where(same, w[k : k + 1, :], weight)
        before = nn(chosen.astype(BF16), earlier)
        place = jnp.where(chosen > 0.0, before, -1.0)
        place_ref[b] = place
        weight_ref[b] = weight
        rows = nn(as_bf16(one_hot(place)), x_ref[b, 0:ntok, :])
        put_rows(rows.astype(BF16), send_ref.at[:, b * CAP : (b + 1) * CAP, :])


def pick_x(zs, x_all):
    blocks, rows, cut = x_all.shape
    ntok = rows - META
    return pl.pallas_call(
        pick_x_kernel,
        grid_spec=pltpu.PrefetchScalarGridSpec(
            num_scalar_prefetch=1,
            grid=(1,),
            in_specs=[whole(x_all.shape)],
            out_specs=[
                whole((32, blocks * CAP, cut)),
                whole((blocks, 16, ntok)),
                whole((blocks, 16, ntok)),
            ],
        ),
        out_shape=[
            pltpu.HBM((32, blocks * CAP, cut), BF16),
            jax.ShapeDtypeStruct((blocks, 16, ntok), F32),
            jax.ShapeDtypeStruct((blocks, 16, ntok), F32),
        ],
        compiler_params=params(),
        name="pick_x",
    )(zs, x_all)


def pick_g_kernel(z_ref, *refs):
    g_refs, (place_ref, weight_ref, send_ref) = refs[:8], refs[8:]
    for shift, g_ref in enumerate(g_refs):
        block = lax.rem(z_ref[0] + 8 - shift, 8)
        hot = one_hot(place_ref[block])
        rows = nn(as_bf16(hot), g_ref[...]) * row_weights(hot, weight_ref[block])
        put_rows(rows.astype(BF16), send_ref.at[:, pl.ds(pl.multiple_of(block * CAP, CAP), CAP), :])


def pick_g(zs, g_blocks, place, weight):
    blocks = place.shape[0]
    ntok, cut = g_blocks[0].shape
    return pl.pallas_call(
        pick_g_kernel,
        grid_spec=pltpu.PrefetchScalarGridSpec(
            num_scalar_prefetch=1,
            grid=(1,),
            in_specs=[whole((ntok, cut))] * 8 + [whole(place.shape), whole(weight.shape)],
            out_specs=whole((32, blocks * CAP, cut)),
        ),
        out_shape=jax.ShapeDtypeStruct((32, blocks * CAP, cut), BF16),
        compiler_params=params(),
        name="pick_g",
    )(zs, *g_blocks, place, weight)


def chunk(ref, e):
    return jnp.concatenate([ref[q * 8 + e] for q in range(4)], axis=0)


def put_chunk(ref, e, rows):
    for q in range(4):
        ref[q * 8 + e] = rows[q * 128 : (q + 1) * 128]


def forward_kernel(x_ref, wg_ref, wu_ref, wd_ref, out_ref, gate_ref, up_ref, hidden_ref):
    cut = x_ref.shape[2]

    def first(e, _):
        at = pl.ds(pl.multiple_of(e * cut, cut), cut)
        x = chunk(x_ref, e)
        gate_ref[...] += nn(x, wg_ref[0, at, :])
        up_ref[...] += nn(x, wu_ref[0, at, :])
        return 0

    gate_ref[...] = jnp.zeros_like(gate_ref)
    up_ref[...] = jnp.zeros_like(up_ref)
    lax.fori_loop(0, 8, first, 0)
    gate = gate_ref[...]
    hidden_ref[...] = (gate * jax.nn.sigmoid(gate) * up_ref[...]).astype(BF16)

    def second(e, _):
        at = pl.ds(pl.multiple_of(e * cut, cut), cut)
        put_chunk(out_ref, e, nn(hidden_ref[...], wd_ref[0, :, at]).astype(BF16))
        return 0

    lax.fori_loop(0, 8, second, 0)


def forward(x_rows, wg, wu, wd):
    rows, ff = 512, wg.shape[2]
    return pl.pallas_call(
        forward_kernel,
        out_shape=[
            jax.ShapeDtypeStruct(x_rows.shape, BF16),
            jax.ShapeDtypeStruct((rows, ff), F32),
            jax.ShapeDtypeStruct((rows, ff), F32),
            jax.ShapeDtypeStruct((rows, ff), BF16),
        ],
        compiler_params=params(),
        cost_estimate=pl.CostEstimate(
            flops=6 * rows * 2048 * ff, bytes_accessed=11 * 2**20, transcendentals=rows * ff
        ),
        name="forward",
    )(x_rows, wg, wu, wd)


def backward_kernel(
    g_ref, gate_ref, up_ref, wg_ref, wu_ref, wd_ref, in_ref, dgate_ref, dup_ref, back_ref
):
    cut = g_ref.shape[2]

    def first(e, _):
        at = pl.ds(pl.multiple_of(e * cut, cut), cut)
        back_ref[...] += nt(chunk(g_ref, e), wd_ref[0, :, at])
        return 0

    back_ref[...] = jnp.zeros_like(back_ref)
    lax.fori_loop(0, 8, first, 0)
    back, gate = back_ref[...], gate_ref[...]
    sigma = jax.nn.sigmoid(gate)
    dgate_ref[...] = (back * up_ref[...] * sigma * (1.0 + gate * (1.0 - sigma))).astype(BF16)
    dup_ref[...] = (back * (gate * sigma)).astype(BF16)

    def second(e, _):
        at = pl.ds(pl.multiple_of(e * cut, cut), cut)
        piece = nt(dgate_ref[...], wg_ref[0, at, :]) + nt(dup_ref[...], wu_ref[0, at, :])
        put_chunk(in_ref, e, piece.astype(BF16))
        return 0

    lax.fori_loop(0, 8, second, 0)


def backward(g_rows, gate, up, wg, wu, wd):
    rows, ff = gate.shape
    return pl.pallas_call(
        backward_kernel,
        out_shape=[
            jax.ShapeDtypeStruct(g_rows.shape, BF16),
            jax.ShapeDtypeStruct((rows, ff), BF16),
            jax.ShapeDtypeStruct((rows, ff), BF16),
        ],
        scratch_shapes=[pltpu.VMEM((rows, ff), F32)],
        compiler_params=params(),
        cost_estimate=pl.CostEstimate(
            flops=6 * rows * 2048 * ff, bytes_accessed=11 * 2**20, transcendentals=rows * ff
        ),
        name="backward",
    )(g_rows, gate, up, wg, wu, wd)


def grads_kernel(x_ref, g_ref, hidden_ref, dgate_ref, dup_ref, gg_ref, gu_ref, gd_ref):
    cut = x_ref.shape[2]

    def step(e, _):
        at = pl.ds(pl.multiple_of(e * cut, cut), cut)
        x = chunk(x_ref, e)
        gg_ref[0, at, :] = tn(x, dgate_ref[...]).astype(BF16)
        gu_ref[0, at, :] = tn(x, dup_ref[...]).astype(BF16)
        gd_ref[0, :, at] = tn(hidden_ref[...], chunk(g_ref, e)).astype(BF16)
        return 0

    lax.fori_loop(0, 8, step, 0)


def grads(x_rows, g_rows, hidden, dgate, dup):
    rows, ff = hidden.shape
    width = 8 * x_rows.shape[2]
    return pl.pallas_call(
        grads_kernel,
        out_shape=[
            jax.ShapeDtypeStruct((1, width, ff), BF16),
            jax.ShapeDtypeStruct((1, width, ff), BF16),
            jax.ShapeDtypeStruct((1, ff, width), BF16),
        ],
        compiler_params=params(),
        cost_estimate=pl.CostEstimate(
            flops=6 * rows * 2048 * ff, bytes_accessed=10 * 2**20, transcendentals=0
        ),
        name="grads",
    )(x_rows, g_rows, hidden, dgate, dup)


def add_rows(place, scale, back):
    hot = one_hot(place)
    rows = jnp.concatenate(
        [back[2 * l].astype(F32) + back[2 * l + 1].astype(F32) for l in range(16)], axis=0
    )
    if scale is not None:
        rows = rows * row_weights(hot, scale)
    hi = rows.astype(BF16)
    low = (rows - hi.astype(F32)).astype(BF16)
    pick = as_bf16(hot)
    return tn(pick, hi) + tn(pick, low)


def join_out_kernel(z_ref, place_ref, weight_ref, back_ref, own_ref, *sum_refs):
    for shift, sum_ref in enumerate((own_ref, *sum_refs)):
        block = lax.rem(z_ref[0] + shift, 8)
        rows = back_ref.at[:, pl.ds(pl.multiple_of(block * CAP, CAP), CAP), :]
        sum_ref[...] = add_rows(place_ref[block], weight_ref[block], rows).astype(sum_ref.dtype)


def join_out(zs, place, weight, back):
    ntok, cut = place.shape[2], back.shape[2]
    shapes = [jax.ShapeDtypeStruct((ntok, cut), F32 if s == 0 else BF16) for s in range(8)]
    return pl.pallas_call(
        join_out_kernel,
        grid_spec=pltpu.PrefetchScalarGridSpec(
            num_scalar_prefetch=1,
            grid=(1,),
            in_specs=[whole(place.shape), whole(weight.shape), whole(back.shape)],
            out_specs=[whole((ntok, cut))] * 8,
        ),
        out_shape=shapes,
        compiler_params=params(),
        name="join_out",
    )(zs, place, weight, back)


def join_in_kernel(place_ref, back_ref, sum_ref):
    eighth = sum_ref.shape[0] // place_ref.shape[0]
    for b in range(place_ref.shape[0]):
        total = add_rows(place_ref[b], None, back_ref.at[:, b * CAP : (b + 1) * CAP, :])
        sum_ref[b * eighth : (b + 1) * eighth] = total.astype(BF16).reshape(eighth, *sum_ref.shape[1:])


def join_in(place, back):
    blocks, _, ntok = place.shape
    return pl.pallas_call(
        join_in_kernel,
        out_shape=jax.ShapeDtypeStruct((blocks * 8, ntok // 8, back.shape[2]), BF16),
        compiler_params=params(),
        name="join_in",
    )(place, back)


def total_kernel(col_ref, *refs):
    parts, pieces, total_ref = refs[:8], refs[8:16], refs[16]
    total = parts[0][...]
    for part in parts[1:]:
        total = total + part[...].astype(F32)
    total_ref[...] = total
    count = pieces[0].shape[0]
    for shift, piece in enumerate(pieces):
        to = lax.rem(col_ref[0] + shift, 8)
        piece[...] = total_ref[pl.ds(pl.multiple_of(to * count, count), count), :].astype(BF16)


def total(col, parts):
    ntok, cut = parts[0].shape
    return pl.pallas_call(
        total_kernel,
        grid_spec=pltpu.PrefetchScalarGridSpec(
            num_scalar_prefetch=1,
            grid=(1,),
            in_specs=[whole((ntok, cut))] * 8,
            out_specs=[whole((ntok // 8, cut))] * 8,
            scratch_shapes=[pltpu.VMEM((ntok, cut), F32)],
        ),
        out_shape=[jax.ShapeDtypeStruct((ntok // 8, cut), BF16)] * 8,
        compiler_params=params(),
        name="total",
    )(col, *parts)


def last_kernel(col_ref, *refs):
    pieces, part_ref, out_ref, in_ref = refs[:8], refs[8], refs[9], refs[10]
    cut = part_ref.shape[2]
    for shift, piece in enumerate(pieces):
        at = lax.rem(col_ref[0] + 8 - shift, 8) * cut
        out_ref[:, pl.ds(pl.multiple_of(at, cut), cut)] = piece[...]
    for e in range(8):
        whole_sum = part_ref[e].astype(F32)
        for z in range(1, 8):
            whole_sum = whole_sum + part_ref[z * 8 + e].astype(F32)
        in_ref[:, e * cut : (e + 1) * cut] = whole_sum.astype(BF16)


def last(col, pieces, parts):
    _, count, cut = parts.shape
    shape = jax.ShapeDtypeStruct((count, 8 * cut), BF16)
    return pl.pallas_call(
        last_kernel,
        grid_spec=pltpu.PrefetchScalarGridSpec(
            num_scalar_prefetch=1,
            grid=(1,),
            in_specs=[whole((count, cut))] * 8 + [whole(parts.shape)],
            out_specs=[whole(shape.shape)] * 2,
        ),
        out_shape=[shape, shape],
        compiler_params=params(),
        name="last",
    )(col, *pieces, parts)


def swap(buffer, axes):
    return lax.all_to_all(buffer, axes, split_axis=0, concat_axis=0, tiled=True)


def spread(arrays, axes, shifts=range(8)):
    return [
        lax.ppermute(arrays[shift], axes, [(i, (i + shift) % 8) for i in range(8)])
        if shift
        else arrays[0]
        for shift in shifts
    ]


def on_device(
    tokens, expert_ids, route_weight, expert_slot, gate_weight, up_weight, down_weight, cotangent
):
    col = lax.axis_index(EX).astype(jnp.int32).reshape(1)
    zs = lax.axis_index("z").astype(jnp.int32).reshape(1)
    x_cut, g_cut = route(
        col, tokens, cotangent, expert_ids.T, route_weight.T, expert_slot.reshape(1, -1)
    )
    x_all = swap(x_cut, ("z",))
    x_send, place, weight = pick_x(zs, x_all)
    g_blocks = spread([g_cut] * 8, ("z",))
    x_rows = swap(x_send, PLANE)
    g_send = pick_g(zs, g_blocks, place, weight)
    g_rows = swap(g_send, PLANE)
    out_send, gate, up, hidden = forward(x_rows, gate_weight, up_weight, down_weight)
    out_back = pltpu.with_memory_space_constraint(swap(out_send, PLANE), pltpu.HBM)
    in_send, dgate, dup = backward(g_rows, gate, up, gate_weight, up_weight, down_weight)
    weight_grads = grads(x_rows, g_rows, hidden, dgate, dup)
    in_send, weight_grads = lax.optimization_barrier((in_send, weight_grads))
    in_back = swap(in_send, PLANE)
    y_parts = spread(join_out(zs, place, weight, out_back), ("z",))
    pieces = total(col, y_parts)
    early = spread(pieces, EX, range(4))
    in_back, early = lax.optimization_barrier((in_back, early))
    dx_part, pieces = lax.optimization_barrier((join_in(place, in_back), pieces))
    pieces = early + spread(pieces, EX, range(4, 8))
    layer_out, input_grad = last(col, pieces, swap(dx_part, ("z", "xh", "y")))
    return layer_out, input_grad, *weight_grads


def solution(mesh):
    fine = Mesh(mesh.devices.reshape(8, 2, 2, 2, 4), ("z", "xl", "core", "xh", "y"))
    rows, every = P(DP, None), P(DP + EX, None)
    half = P(DP + EX, None, None)
    return jax.shard_map(
        on_device,
        mesh=fine,
        in_specs=(rows, rows, rows, P(), half, half, half, rows),
        out_specs=(every, every, half, half, half),
        check_vma=False,
    )
```

```python
import jax
import jax.numpy as jnp
from jax import lax
from jax.experimental import pallas as pl
from jax.experimental.pallas import tpu as pltpu
from jax.sharding import Mesh, PartitionSpec as P

DP = ("z", "xl", "core")
EX = ("xh", "y")
PLANE = ("xl", "core", "xh", "y")
BF16 = jnp.bfloat16
F32 = jnp.float32
CAP = 16
EARLY = (1, 2, 4, 6, 7)
META = 16


def nn(a, b):
    return lax.dot_general(a, b, (((1,), (0,)), ((), ())), preferred_element_type=F32)


def nt(a, b):
    return lax.dot_general(a, b, (((1,), (1,)), ((), ())), preferred_element_type=F32)


def tn(a, b):
    return lax.dot_general(a, b, (((0,), (0,)), ((), ())), preferred_element_type=F32)


def params(mib=16):
    return pltpu.CompilerParams(vmem_limit_bytes=mib * 2**20)


def whole(shape):
    return pl.BlockSpec(shape, lambda *_: (0,) * len(shape))


def route_kernel(col_ref, tok_ref, ids_ref, rw_ref, slot_ref, x_ref, slots_ref):
    ntok = tok_ref.shape[0]
    table = jnp.broadcast_to(slot_ref[...], (8, slot_ref.shape[1]))
    slots = jnp.take_along_axis(table, ids_ref[...], axis=1, mode="promise_in_bounds").astype(F32)
    slots_ref[...] = slots
    w = rw_ref[...]
    hi = w.astype(BF16).astype(F32)
    rest = w - hi
    mid = rest.astype(BF16).astype(F32)
    low = rest - mid
    tok = tok_ref[...]
    left = jnp.concatenate([slots, mid], axis=0).astype(BF16)
    right = jnp.concatenate([hi, low], axis=0).astype(BF16)
    for z in range(x_ref.shape[0]):
        x_ref[z, 0:ntok, :] = tok
        x_ref[z, ntok : ntok + META, 0:128] = left
        x_ref[z, ntok : ntok + META, 128:256] = right


def route(col, tokens, ids_t, rw_t, slot_row):
    ntok, width = tokens.shape
    cut = width // 8
    return pl.pallas_call(
        route_kernel,
        grid_spec=pltpu.PrefetchScalarGridSpec(
            num_scalar_prefetch=1,
            grid=(1,),
            in_specs=[
                pl.BlockSpec((ntok, cut), lambda i, c: (0, c[0])),
                whole(ids_t.shape),
                whole(rw_t.shape),
                whole(slot_row.shape),
            ],
            out_specs=[whole((8, ntok + META, cut)), whole(ids_t.shape)],
        ),
        out_shape=[
            jax.ShapeDtypeStruct((8, ntok + META, cut), BF16),
            jax.ShapeDtypeStruct(ids_t.shape, F32),
        ],
        compiler_params=params(60),
        name="route",
    )(col, tokens, ids_t, rw_t, slot_row)


def one_hot(place):
    slots, ntok = place.shape
    spread = jnp.broadcast_to(place[:, None, :], (slots, CAP, ntok)).reshape(slots * CAP, ntok)
    at = lax.broadcasted_iota(jnp.int32, (slots * CAP, ntok), 0) % CAP
    return spread == at.astype(F32)


def row_weights(hot, weight):
    slots, ntok = weight.shape
    spread = jnp.broadcast_to(weight[:, None, :], (slots, CAP, ntok)).reshape(slots * CAP, ntok)
    return jnp.sum(jnp.where(hot, spread, 0.0), axis=1, keepdims=True)


def as_bf16(hot):
    return jnp.where(hot, 1.0, 0.0).astype(BF16)


def put_rows(rows, send_ref):
    for l in range(rows.shape[0] // CAP):
        part = rows[l * CAP : (l + 1) * CAP]
        send_ref[2 * l] = part
        send_ref[2 * l + 1] = part


def places(slots, w, local, earlier):
    chosen = jnp.zeros(local.shape, F32)
    weight = jnp.zeros(local.shape, F32)
    for k in range(8):
        same = local == slots[k : k + 1, :]
        chosen = jnp.where(same, 1.0, chosen)
        weight = jnp.where(same, w[k : k + 1, :], weight)
    before = nn(chosen.astype(BF16), earlier)
    return jnp.where(chosen > 0.0, before, -1.0), weight


def earlier_tokens(ntok):
    row = lax.broadcasted_iota(jnp.int32, (ntok, ntok), 0)
    column = lax.broadcasted_iota(jnp.int32, (ntok, ntok), 1)
    return jnp.where(row < column, 1.0, 0.0).astype(BF16)


def pick_x_kernel(at_ref, x_ref, send_ref, place_ref, weight_ref):
    ntok = x_ref.shape[1] - META
    first = (at_ref[0] * 16).astype(F32)
    local = lax.broadcasted_iota(jnp.int32, (16, ntok), 0).astype(F32) + first
    earlier = earlier_tokens(ntok)
    for b in range(x_ref.shape[0]):
        left = x_ref[b, ntok : ntok + META, 0:128].astype(F32)
        right = x_ref[b, ntok : ntok + META, 128:256].astype(F32)
        w = right[0:8] + left[8:16] + right[8:16]
        place, weight = places(left[0:8], w, local, earlier)
        place_ref[b] = place
        weight_ref[b] = weight
        rows = nn(as_bf16(one_hot(place)), x_ref[b, 0:ntok, :])
        put_rows(rows.astype(BF16), send_ref.at[:, b * CAP : (b + 1) * CAP, :])


def pick_x(zs, x_all):
    blocks, rows, cut = x_all.shape
    ntok = rows - META
    return pl.pallas_call(
        pick_x_kernel,
        grid_spec=pltpu.PrefetchScalarGridSpec(
            num_scalar_prefetch=1,
            grid=(1,),
            in_specs=[whole(x_all.shape)],
            out_specs=[
                whole((32, blocks * CAP, cut)),
                whole((blocks, 16, ntok)),
                whole((blocks, 16, ntok)),
            ],
        ),
        out_shape=[
            pltpu.HBM((32, blocks * CAP, cut), BF16),
            jax.ShapeDtypeStruct((blocks, 16, ntok), F32),
            jax.ShapeDtypeStruct((blocks, 16, ntok), F32),
        ],
        compiler_params=params(),
        name="pick_x",
    )(zs, x_all)


ROUTES = ((0, 0), (1, 0), (2, 0), (2, 1), (3, 0), (3, 1))


def pick_g_kernel(at_ref, cot_ref, slots_ref, rw_ref, *send_refs):
    ntok, width = cot_ref.shape
    earlier = earlier_tokens(ntok)
    planes = lax.broadcasted_iota(jnp.int32, (8, ntok), 0)
    for (away, over), send_ref in zip(ROUTES, send_refs):
        local = planes * 16 + ((at_ref[1] ^ away) * 4 + ((at_ref[2] // 2) ^ (2 * over)))
        place, weight = places(slots_ref[...], rw_ref[...], local.astype(F32), earlier)
        hot = one_hot(place)
        pick, scale = as_bf16(hot), row_weights(hot, weight)
        begin = over * (width // 2)
        for c in range(0, send_ref.shape[1], 512):
            rows = nn(pick, cot_ref[:, begin + c : begin + c + 512]) * scale
            send_ref[:, c : c + 512] = rows.astype(BF16)


def pick_g(at, cotangent, slots, rw_t):
    ntok, width = cotangent.shape
    shapes = [(8 * CAP, width if away < 2 else width // 2) for away, _ in ROUTES]
    return pl.pallas_call(
        pick_g_kernel,
        grid_spec=pltpu.PrefetchScalarGridSpec(
            num_scalar_prefetch=1,
            grid=(1,),
            in_specs=[whole(cotangent.shape), whole(slots.shape), whole(rw_t.shape)],
            out_specs=[whole(shape) for shape in shapes],
        ),
        out_shape=[jax.ShapeDtypeStruct(shape, BF16) for shape in shapes],
        compiler_params=params(),
        name="pick_g",
    )(at, cotangent, slots, rw_t)


def turn_g_kernel(at_ref, *refs):
    given, send_refs = refs[: len(ROUTES)], refs[len(ROUTES) :]
    for shift, send_ref in enumerate(send_refs):
        to = pl.ds(pl.multiple_of(lax.rem(at_ref[0] + shift, 8) * CAP, CAP), CAP)
        for (away, over), rows in zip(ROUTES, given):
            begin, count = over * (send_ref.shape[1] // 2), rows.shape[1]
            send_ref[away * CAP : (away + 1) * CAP, begin : begin + count] = rows[to, :]


def turn_g(at, given):
    width = given[0].shape[1]
    return pl.pallas_call(
        turn_g_kernel,
        grid_spec=pltpu.PrefetchScalarGridSpec(
            num_scalar_prefetch=1,
            grid=(1,),
            in_specs=[whole(a.shape) for a in given],
            out_specs=[whole((4 * CAP, width))] * 8,
        ),
        out_shape=[pltpu.HBM((4 * CAP, width), BF16)] * 8,
        compiler_params=params(),
        name="turn_g",
    )(at, *given)


def chunk(ref, e):
    return jnp.concatenate([ref[q * 8 + e] for q in range(4)], axis=0)


def columns(ref, at):
    return jnp.concatenate([ref[q, :, at] for q in range(4)], axis=0)


def put_chunk(ref, e, rows):
    for q in range(4):
        ref[q * 8 + e] = rows[q * 128 : (q + 1) * 128]


def forward_kernel(x_ref, wg_ref, wu_ref, wd_ref, out_ref, gate_ref, up_ref, hidden_ref):
    cut = x_ref.shape[2]

    def first(e, _):
        at = pl.ds(pl.multiple_of(e * cut, cut), cut)
        x = chunk(x_ref, e)
        gate_ref[...] += nn(x, wg_ref[0, at, :])
        up_ref[...] += nn(x, wu_ref[0, at, :])
        return 0

    gate_ref[...] = jnp.zeros_like(gate_ref)
    up_ref[...] = jnp.zeros_like(up_ref)
    lax.fori_loop(0, 8, first, 0)
    gate = gate_ref[...]
    hidden_ref[...] = (gate * jax.nn.sigmoid(gate) * up_ref[...]).astype(BF16)

    def second(e, _):
        at = pl.ds(pl.multiple_of(e * cut, cut), cut)
        put_chunk(out_ref, e, nn(hidden_ref[...], wd_ref[0, :, at]).astype(BF16))
        return 0

    lax.fori_loop(0, 8, second, 0)


def forward(x_rows, wg, wu, wd):
    rows, ff = 512, wg.shape[2]
    return pl.pallas_call(
        forward_kernel,
        out_shape=[
            jax.ShapeDtypeStruct(x_rows.shape, BF16),
            jax.ShapeDtypeStruct((rows, ff), F32),
            jax.ShapeDtypeStruct((rows, ff), F32),
            jax.ShapeDtypeStruct((rows, ff), BF16),
        ],
        compiler_params=params(),
        cost_estimate=pl.CostEstimate(
            flops=6 * rows * 2048 * ff, bytes_accessed=11 * 2**20, transcendentals=rows * ff
        ),
        name="forward",
    )(x_rows, wg, wu, wd)


def backward_kernel(at_ref, *refs):
    parts, (gate_ref, up_ref, wg_ref, wu_ref, wd_ref) = refs[:8], refs[8:13]
    g_ref, in_ref, dgate_ref, dup_ref, back_ref = refs[13:]
    cut = in_ref.shape[2]
    for shift, part in enumerate(parts):
        rows = pl.ds(pl.multiple_of(lax.rem(at_ref[0] + 8 - shift, 8) * CAP, CAP), CAP)
        for away in range(4):
            g_ref[at_ref[1] ^ away, rows, :] = part[away * CAP : (away + 1) * CAP, :]

    def first(e, _):
        at = pl.ds(pl.multiple_of(e * cut, cut), cut)
        back_ref[...] += nt(columns(g_ref, at), wd_ref[0, :, at])
        return 0

    back_ref[...] = jnp.zeros_like(back_ref)
    lax.fori_loop(0, 8, first, 0)
    back, gate = back_ref[...], gate_ref[...]
    sigma = jax.nn.sigmoid(gate)
    dgate_ref[...] = (back * up_ref[...] * sigma * (1.0 + gate * (1.0 - sigma))).astype(BF16)
    dup_ref[...] = (back * (gate * sigma)).astype(BF16)

    def second(e, _):
        at = pl.ds(pl.multiple_of(e * cut, cut), cut)
        piece = nt(dgate_ref[...], wg_ref[0, at, :]) + nt(dup_ref[...], wu_ref[0, at, :])
        put_chunk(in_ref, e, piece.astype(BF16))
        return 0

    lax.fori_loop(0, 8, second, 0)


def backward(at, parts, gate, up, wg, wu, wd):
    rows, ff = gate.shape
    width = wd.shape[2]
    return pl.pallas_call(
        backward_kernel,
        grid_spec=pltpu.PrefetchScalarGridSpec(
            num_scalar_prefetch=1,
            grid=(1,),
            in_specs=[whole(a.shape) for a in (*parts, gate, up, wg, wu, wd)],
            out_specs=[
                whole((4, rows // 4, width)),
                whole((32, rows // 4, width // 8)),
                whole((rows, ff)),
                whole((rows, ff)),
            ],
            scratch_shapes=[pltpu.VMEM((rows, ff), F32)],
        ),
        out_shape=[
            jax.ShapeDtypeStruct((4, rows // 4, width), BF16),
            jax.ShapeDtypeStruct((32, rows // 4, width // 8), BF16),
            jax.ShapeDtypeStruct((rows, ff), BF16),
            jax.ShapeDtypeStruct((rows, ff), BF16),
        ],
        compiler_params=params(36),
        cost_estimate=pl.CostEstimate(
            flops=6 * rows * 2048 * ff, bytes_accessed=13 * 2**20, transcendentals=rows * ff
        ),
        name="backward",
    )(at, *parts, gate, up, wg, wu, wd)


def grads_kernel(x_ref, g_ref, hidden_ref, dgate_ref, dup_ref, gg_ref, gu_ref, gd_ref):
    cut = x_ref.shape[2]

    def step(e, _):
        at = pl.ds(pl.multiple_of(e * cut, cut), cut)
        x = chunk(x_ref, e)
        gg_ref[0, at, :] = tn(x, dgate_ref[...]).astype(BF16)
        gu_ref[0, at, :] = tn(x, dup_ref[...]).astype(BF16)
        gd_ref[0, :, at] = tn(hidden_ref[...], columns(g_ref, at)).astype(BF16)
        return 0

    lax.fori_loop(0, 8, step, 0)


def grads(x_rows, g_rows, hidden, dgate, dup):
    rows, ff = hidden.shape
    width = 8 * x_rows.shape[2]
    return pl.pallas_call(
        grads_kernel,
        out_shape=[
            jax.ShapeDtypeStruct((1, width, ff), BF16),
            jax.ShapeDtypeStruct((1, width, ff), BF16),
            jax.ShapeDtypeStruct((1, ff, width), BF16),
        ],
        compiler_params=params(),
        cost_estimate=pl.CostEstimate(
            flops=6 * rows * 2048 * ff, bytes_accessed=10 * 2**20, transcendentals=0
        ),
        name="grads",
    )(x_rows, g_rows, hidden, dgate, dup)


def add_rows(place, scale, back):
    hot = one_hot(place)
    rows = jnp.concatenate(
        [back[2 * l].astype(F32) + back[2 * l + 1].astype(F32) for l in range(16)], axis=0
    )
    if scale is not None:
        rows = rows * row_weights(hot, scale)
    hi = rows.astype(BF16)
    low = (rows - hi.astype(F32)).astype(BF16)
    pick = as_bf16(hot)
    return tn(pick, hi) + tn(pick, low)


def join_out_kernel(z_ref, place_ref, weight_ref, back_ref, own_ref, *sum_refs):
    for shift, sum_ref in enumerate((own_ref, *sum_refs)):
        block = lax.rem(z_ref[0] + shift, 8)
        rows = back_ref.at[:, pl.ds(pl.multiple_of(block * CAP, CAP), CAP), :]
        sum_ref[...] = add_rows(place_ref[block], weight_ref[block], rows).astype(sum_ref.dtype)


def join_out(zs, place, weight, back):
    ntok, cut = place.shape[2], back.shape[2]
    shapes = [jax.ShapeDtypeStruct((ntok, cut), F32 if s == 0 else BF16) for s in range(8)]
    return pl.pallas_call(
        join_out_kernel,
        grid_spec=pltpu.PrefetchScalarGridSpec(
            num_scalar_prefetch=1,
            grid=(1,),
            in_specs=[whole(place.shape), whole(weight.shape), whole(back.shape)],
            out_specs=[whole((ntok, cut))] * 8,
        ),
        out_shape=shapes,
        compiler_params=params(),
        name="join_out",
    )(zs, place, weight, back)


def join_in_kernel(place_ref, back_ref, sum_ref):
    eighth = sum_ref.shape[0] // place_ref.shape[0]
    for b in range(place_ref.shape[0]):
        total = add_rows(place_ref[b], None, back_ref.at[:, b * CAP : (b + 1) * CAP, :])
        sum_ref[b * eighth : (b + 1) * eighth] = total.astype(BF16).reshape(eighth, *sum_ref.shape[1:])


def join_in(place, back):
    blocks, _, ntok = place.shape
    return pl.pallas_call(
        join_in_kernel,
        out_shape=jax.ShapeDtypeStruct((blocks * 8, ntok // 8, back.shape[2]), BF16),
        compiler_params=params(),
        name="join_in",
    )(place, back)


def total_kernel(col_ref, *refs):
    parts, pieces, total_ref = refs[:8], refs[8:16], refs[16]
    total = parts[0][...]
    for part in parts[1:]:
        total = total + part[...].astype(F32)
    total_ref[...] = total
    count = pieces[0].shape[0]
    for shift, piece in enumerate(pieces):
        to = lax.rem(col_ref[0] + shift, 8)
        piece[...] = total_ref[pl.ds(pl.multiple_of(to * count, count), count), :].astype(BF16)


def total(col, parts):
    ntok, cut = parts[0].shape
    return pl.pallas_call(
        total_kernel,
        grid_spec=pltpu.PrefetchScalarGridSpec(
            num_scalar_prefetch=1,
            grid=(1,),
            in_specs=[whole((ntok, cut))] * 8,
            out_specs=[whole((ntok // 8, cut))] * 8,
            scratch_shapes=[pltpu.VMEM((ntok, cut), F32)],
        ),
        out_shape=[jax.ShapeDtypeStruct((ntok // 8, cut), BF16)] * 8,
        compiler_params=params(),
        name="total",
    )(col, *parts)


def last_kernel(col_ref, *refs):
    pieces, part_ref, out_ref, in_ref = refs[:8], refs[8], refs[9], refs[10]
    cut = part_ref.shape[2]
    for shift, piece in enumerate(pieces):
        at = lax.rem(col_ref[0] + 8 - shift, 8) * cut
        out_ref[:, pl.ds(pl.multiple_of(at, cut), cut)] = piece[...]
    for e in range(8):
        whole_sum = part_ref[e].astype(F32)
        for z in range(1, 8):
            whole_sum = whole_sum + part_ref[z * 8 + e].astype(F32)
        in_ref[:, e * cut : (e + 1) * cut] = whole_sum.astype(BF16)


def last(col, pieces, parts):
    _, count, cut = parts.shape
    shape = jax.ShapeDtypeStruct((count, 8 * cut), BF16)
    return pl.pallas_call(
        last_kernel,
        grid_spec=pltpu.PrefetchScalarGridSpec(
            num_scalar_prefetch=1,
            grid=(1,),
            in_specs=[whole((count, cut))] * 8 + [whole(parts.shape)],
            out_specs=[whole(shape.shape)] * 2,
        ),
        out_shape=[shape, shape],
        compiler_params=params(),
        name="last",
    )(col, *pieces, parts)


def swap(buffer, axes):
    return lax.all_to_all(buffer, axes, split_axis=0, concat_axis=0, tiled=True)


def spread(arrays, axes):
    return [arrays[0]] + [
        lax.ppermute(arrays[shift], axes, [(i, (i + shift) % 8) for i in range(8)])
        for shift in range(1, 8)
    ]


def in_hbm(array):
    return pltpu.with_memory_space_constraint(array, pltpu.HBM)


def after(value, others):
    return lax.optimization_barrier((value, others))[0]


def cross(arrays):
    return [arrays[0]] + [
        lax.ppermute(
            array, ("xl", "core", "xh"), [(i, i ^ (2 * away + over)) for i in range(8)]
        )
        for (away, over), array in zip(ROUTES[1:], arrays[1:])
    ]


def on_device(
    tokens, expert_ids, route_weight, expert_slot, gate_weight, up_weight, down_weight, cotangent
):
    col = lax.axis_index(EX).astype(jnp.int32).reshape(1)
    zs = lax.axis_index("z").astype(jnp.int32).reshape(1)
    at = jnp.concatenate([zs, lax.axis_index(("xl", "core")).astype(jnp.int32).reshape(1), col])
    rw_t = route_weight.T
    x_cut, slots = route(col, tokens, expert_ids.T, rw_t, expert_slot.reshape(1, -1))
    x_all = swap(x_cut, ("z",))
    g_crossed = cross(pick_g(at, cotangent, slots, rw_t))
    x_all = after(x_all, g_crossed)
    g_turned = turn_g(at, g_crossed)
    g_parts = [in_hbm(part) for part in spread(g_turned, ("z",))]
    x_send, place, weight = pick_x(zs, x_all)
    x_rows = after(swap(x_send, PLANE), g_turned)
    out_send, gate, up, hidden = forward(x_rows, gate_weight, up_weight, down_weight)
    out_send = after(out_send, [g_parts[s] for s in EARLY])
    out_back = in_hbm(swap(out_send, PLANE))
    g_rows, in_send, dgate, dup = backward(
        at, g_parts, gate, up, gate_weight, up_weight, down_weight
    )
    weight_grads = grads(x_rows, g_rows, hidden, dgate, dup)
    in_send, weight_grads = lax.optimization_barrier((in_send, weight_grads))
    in_back = swap(in_send, PLANE)
    y_parts = spread(join_out(zs, place, weight, out_back), ("z",))
    pieces = total(col, y_parts)
    in_back, pieces = lax.optimization_barrier((in_back, pieces))
    dx_part = join_in(place, in_back)
    pieces = spread(pieces, EX)
    layer_out, input_grad = last(col, pieces, swap(dx_part, ("z", "xh", "y")))
    return layer_out, input_grad, *weight_grads


def solution(mesh):
    fine = Mesh(mesh.devices.reshape(8, 2, 2, 2, 4), ("z", "xl", "core", "xh", "y"))
    rows, every = P(DP, None), P(DP + EX, None)
    half = P(DP + EX, None, None)
    return jax.shard_map(
        on_device,
        mesh=fine,
        in_specs=(rows, rows, rows, P(), half, half, half, rows),
        out_specs=(every, every, half, half, half),
        check_vma=False,
    )
```

```python
import jax
import jax.numpy as jnp
from jax import lax
from jax.experimental import pallas as pl
from jax.experimental.pallas import tpu as pltpu
from jax.sharding import Mesh, PartitionSpec as P

DP = ("z", "xl", "core")
EX = ("xh", "y")
PLANE = ("xl", "core", "xh", "y")
BF16 = jnp.bfloat16
F32 = jnp.float32
CAP = 16
EARLY = (1, 2, 3, 5, 6, 7)
META = 16


def nn(a, b):
    return lax.dot_general(a, b, (((1,), (0,)), ((), ())), preferred_element_type=F32)


def nt(a, b):
    return lax.dot_general(a, b, (((1,), (1,)), ((), ())), preferred_element_type=F32)


def tn(a, b):
    return lax.dot_general(a, b, (((0,), (0,)), ((), ())), preferred_element_type=F32)


def params(mib=16):
    return pltpu.CompilerParams(vmem_limit_bytes=mib * 2**20)


def whole(shape):
    return pl.BlockSpec(shape, lambda *_: (0,) * len(shape))


def route_kernel(col_ref, tok_ref, ids_ref, rw_ref, slot_ref, x_ref, slots_ref):
    ntok = tok_ref.shape[0]
    table = jnp.broadcast_to(slot_ref[...], (8, slot_ref.shape[1]))
    slots = jnp.take_along_axis(table, ids_ref[...], axis=1, mode="promise_in_bounds").astype(F32)
    slots_ref[...] = slots
    w = rw_ref[...]
    hi = w.astype(BF16).astype(F32)
    rest = w - hi
    mid = rest.astype(BF16).astype(F32)
    low = rest - mid
    tok = tok_ref[...]
    left = jnp.concatenate([slots, mid], axis=0).astype(BF16)
    right = jnp.concatenate([hi, low], axis=0).astype(BF16)
    for z in range(x_ref.shape[0]):
        x_ref[z, 0:ntok, :] = tok
        x_ref[z, ntok : ntok + META, 0:128] = left
        x_ref[z, ntok : ntok + META, 128:256] = right


def route(col, tokens, ids_t, rw_t, slot_row):
    ntok, width = tokens.shape
    cut = width // 8
    return pl.pallas_call(
        route_kernel,
        grid_spec=pltpu.PrefetchScalarGridSpec(
            num_scalar_prefetch=1,
            grid=(1,),
            in_specs=[
                pl.BlockSpec((ntok, cut), lambda i, c: (0, c[0])),
                whole(ids_t.shape),
                whole(rw_t.shape),
                whole(slot_row.shape),
            ],
            out_specs=[whole((8, ntok + META, cut)), whole(ids_t.shape)],
        ),
        out_shape=[
            jax.ShapeDtypeStruct((8, ntok + META, cut), BF16),
            jax.ShapeDtypeStruct(ids_t.shape, F32),
        ],
        compiler_params=params(60),
        name="route",
    )(col, tokens, ids_t, rw_t, slot_row)


def one_hot(place):
    slots, ntok = place.shape
    spread = jnp.broadcast_to(place[:, None, :], (slots, CAP, ntok)).reshape(slots * CAP, ntok)
    at = lax.broadcasted_iota(jnp.int32, (slots * CAP, ntok), 0) % CAP
    return spread == at.astype(F32)


def row_weights(hot, weight):
    slots, ntok = weight.shape
    spread = jnp.broadcast_to(weight[:, None, :], (slots, CAP, ntok)).reshape(slots * CAP, ntok)
    return jnp.sum(jnp.where(hot, spread, 0.0), axis=1, keepdims=True)


def as_bf16(hot):
    return jnp.where(hot, 1.0, 0.0).astype(BF16)


def put_rows(rows, send_ref):
    for l in range(rows.shape[0] // CAP):
        part = rows[l * CAP : (l + 1) * CAP]
        send_ref[2 * l] = part
        send_ref[2 * l + 1] = part


def places(slots, w, local, earlier):
    chosen = jnp.zeros(local.shape, F32)
    weight = jnp.zeros(local.shape, F32)
    for k in range(8):
        same = local == slots[k : k + 1, :]
        chosen = jnp.where(same, 1.0, chosen)
        weight = jnp.where(same, w[k : k + 1, :], weight)
    before = nn(chosen.astype(BF16), earlier)
    return jnp.where(chosen > 0.0, before, -1.0), weight


def earlier_tokens(ntok):
    row = lax.broadcasted_iota(jnp.int32, (ntok, ntok), 0)
    column = lax.broadcasted_iota(jnp.int32, (ntok, ntok), 1)
    return jnp.where(row < column, 1.0, 0.0).astype(BF16)


def pick_x_kernel(at_ref, x_ref, send_ref, place_ref, weight_ref):
    ntok = x_ref.shape[1] - META
    first = (at_ref[0] * 16).astype(F32)
    local = lax.broadcasted_iota(jnp.int32, (16, ntok), 0).astype(F32) + first
    earlier = earlier_tokens(ntok)
    for b in range(x_ref.shape[0]):
        left = x_ref[b, ntok : ntok + META, 0:128].astype(F32)
        right = x_ref[b, ntok : ntok + META, 128:256].astype(F32)
        w = right[0:8] + left[8:16] + right[8:16]
        place, weight = places(left[0:8], w, local, earlier)
        place_ref[b] = place
        weight_ref[b] = weight
        rows = nn(as_bf16(one_hot(place)), x_ref[b, 0:ntok, :])
        put_rows(rows.astype(BF16), send_ref.at[:, b * CAP : (b + 1) * CAP, :])


def pick_x(zs, x_all):
    blocks, rows, cut = x_all.shape
    ntok = rows - META
    return pl.pallas_call(
        pick_x_kernel,
        grid_spec=pltpu.PrefetchScalarGridSpec(
            num_scalar_prefetch=1,
            grid=(1,),
            in_specs=[whole(x_all.shape)],
            out_specs=[
                whole((32, blocks * CAP, cut)),
                whole((blocks, 16, ntok)),
                whole((blocks, 16, ntok)),
            ],
        ),
        out_shape=[
            pltpu.HBM((32, blocks * CAP, cut), BF16),
            jax.ShapeDtypeStruct((blocks, 16, ntok), F32),
            jax.ShapeDtypeStruct((blocks, 16, ntok), F32),
        ],
        compiler_params=params(),
        name="pick_x",
    )(zs, x_all)


ROUTES = ((0, 0), (1, 0), (2, 0), (2, 1), (3, 0), (3, 1))


def pick_g_kernel(at_ref, cot_ref, slots_ref, rw_ref, *send_refs):
    ntok, width = cot_ref.shape
    earlier = earlier_tokens(ntok)
    planes = lax.broadcasted_iota(jnp.int32, (8, ntok), 0)
    for (away, over), send_ref in zip(ROUTES, send_refs):
        local = planes * 16 + ((at_ref[1] ^ away) * 4 + ((at_ref[2] // 2) ^ (2 * over)))
        place, weight = places(slots_ref[...], rw_ref[...], local.astype(F32), earlier)
        hot = one_hot(place)
        pick, scale = as_bf16(hot), row_weights(hot, weight)
        begin = over * (width // 2)
        for c in range(0, send_ref.shape[1], 512):
            rows = nn(pick, cot_ref[:, begin + c : begin + c + 512]) * scale
            send_ref[:, c : c + 512] = rows.astype(BF16)


def pick_g(at, cotangent, slots, rw_t):
    ntok, width = cotangent.shape
    shapes = [(8 * CAP, width if away < 2 else width // 2) for away, _ in ROUTES]
    return pl.pallas_call(
        pick_g_kernel,
        grid_spec=pltpu.PrefetchScalarGridSpec(
            num_scalar_prefetch=1,
            grid=(1,),
            in_specs=[whole(cotangent.shape), whole(slots.shape), whole(rw_t.shape)],
            out_specs=[whole(shape) for shape in shapes],
        ),
        out_shape=[jax.ShapeDtypeStruct(shape, BF16) for shape in shapes],
        compiler_params=params(),
        name="pick_g",
    )(at, cotangent, slots, rw_t)


def turn_g_kernel(at_ref, *refs):
    given, send_refs = refs[: len(ROUTES)], refs[len(ROUTES) :]
    for shift, send_ref in enumerate(send_refs):
        to = pl.ds(pl.multiple_of(lax.rem(at_ref[0] + shift, 8) * CAP, CAP), CAP)
        for (away, over), rows in zip(ROUTES, given):
            begin, count = over * (send_ref.shape[1] // 2), rows.shape[1]
            send_ref[away * CAP : (away + 1) * CAP, begin : begin + count] = rows[to, :]


def turn_g(at, given):
    width = given[0].shape[1]
    return pl.pallas_call(
        turn_g_kernel,
        grid_spec=pltpu.PrefetchScalarGridSpec(
            num_scalar_prefetch=1,
            grid=(1,),
            in_specs=[whole(a.shape) for a in given],
            out_specs=[whole((4 * CAP, width))] * 8,
        ),
        out_shape=[pltpu.HBM((4 * CAP, width), BF16)] * 8,
        compiler_params=params(),
        name="turn_g",
    )(at, *given)


def chunk(ref, e):
    return jnp.concatenate([ref[q * 8 + e] for q in range(4)], axis=0)


def columns(ref, at):
    return jnp.concatenate([ref[q, :, at] for q in range(4)], axis=0)


def put_chunk(ref, e, rows):
    for q in range(4):
        ref[q * 8 + e] = rows[q * 128 : (q + 1) * 128]


def forward_kernel(x_ref, wg_ref, wu_ref, wd_ref, out_ref, gate_ref, up_ref, hidden_ref):
    cut = x_ref.shape[2]

    def first(e, _):
        at = pl.ds(pl.multiple_of(e * cut, cut), cut)
        x = chunk(x_ref, e)
        gate_ref[...] += nn(x, wg_ref[0, at, :])
        up_ref[...] += nn(x, wu_ref[0, at, :])
        return 0

    gate_ref[...] = jnp.zeros_like(gate_ref)
    up_ref[...] = jnp.zeros_like(up_ref)
    lax.fori_loop(0, 8, first, 0)
    gate = gate_ref[...]
    hidden_ref[...] = (gate * jax.nn.sigmoid(gate) * up_ref[...]).astype(BF16)

    def second(e, _):
        at = pl.ds(pl.multiple_of(e * cut, cut), cut)
        put_chunk(out_ref, e, nn(hidden_ref[...], wd_ref[0, :, at]).astype(BF16))
        return 0

    lax.fori_loop(0, 8, second, 0)


def forward(x_rows, wg, wu, wd):
    rows, ff = 512, wg.shape[2]
    return pl.pallas_call(
        forward_kernel,
        out_shape=[
            pltpu.HBM(x_rows.shape, BF16),
            pltpu.HBM((rows, ff), F32),
            pltpu.HBM((rows, ff), F32),
            pltpu.HBM((rows, ff), BF16),
        ],
        compiler_params=params(),
        cost_estimate=pl.CostEstimate(
            flops=6 * rows * 2048 * ff, bytes_accessed=11 * 2**20, transcendentals=rows * ff
        ),
        name="forward",
    )(x_rows, wg, wu, wd)


def backward_kernel(at_ref, *refs):
    parts, (gate_ref, up_ref, wg_ref, wu_ref, wd_ref) = refs[:8], refs[8:13]
    g_ref, in_ref, dgate_ref, dup_ref, back_ref = refs[13:]
    cut = in_ref.shape[2]
    for shift, part in enumerate(parts):
        rows = pl.ds(pl.multiple_of(lax.rem(at_ref[0] + 8 - shift, 8) * CAP, CAP), CAP)
        for away in range(4):
            g_ref[at_ref[1] ^ away, rows, :] = part[away * CAP : (away + 1) * CAP, :]

    def first(e, _):
        at = pl.ds(pl.multiple_of(e * cut, cut), cut)
        back_ref[...] += nt(columns(g_ref, at), wd_ref[0, :, at])
        return 0

    back_ref[...] = jnp.zeros_like(back_ref)
    lax.fori_loop(0, 8, first, 0)
    back, gate = back_ref[...], gate_ref[...]
    sigma = jax.nn.sigmoid(gate)
    dgate_ref[...] = (back * up_ref[...] * sigma * (1.0 + gate * (1.0 - sigma))).astype(BF16)
    dup_ref[...] = (back * (gate * sigma)).astype(BF16)

    def second(e, _):
        at = pl.ds(pl.multiple_of(e * cut, cut), cut)
        piece = nt(dgate_ref[...], wg_ref[0, at, :]) + nt(dup_ref[...], wu_ref[0, at, :])
        put_chunk(in_ref, e, piece.astype(BF16))
        return 0

    lax.fori_loop(0, 8, second, 0)


def backward(at, parts, gate, up, wg, wu, wd):
    rows, ff = gate.shape
    width = wd.shape[2]
    return pl.pallas_call(
        backward_kernel,
        grid_spec=pltpu.PrefetchScalarGridSpec(
            num_scalar_prefetch=1,
            grid=(1,),
            in_specs=[whole(a.shape) for a in (*parts, gate, up, wg, wu, wd)],
            out_specs=[
                whole((4, rows // 4, width)),
                whole((32, rows // 4, width // 8)),
                whole((rows, ff)),
                whole((rows, ff)),
            ],
            scratch_shapes=[pltpu.VMEM((rows, ff), F32)],
        ),
        out_shape=[
            pltpu.HBM((4, rows // 4, width), BF16),
            pltpu.HBM((32, rows // 4, width // 8), BF16),
            pltpu.HBM((rows, ff), BF16),
            pltpu.HBM((rows, ff), BF16),
        ],
        compiler_params=params(36),
        cost_estimate=pl.CostEstimate(
            flops=6 * rows * 2048 * ff, bytes_accessed=13 * 2**20, transcendentals=rows * ff
        ),
        name="backward",
    )(at, *parts, gate, up, wg, wu, wd)


def grads_kernel(x_ref, g_ref, hidden_ref, dgate_ref, dup_ref, gg_ref, gu_ref, gd_ref):
    cut = x_ref.shape[2]

    def step(e, _):
        at = pl.ds(pl.multiple_of(e * cut, cut), cut)
        x = chunk(x_ref, e)
        gg_ref[0, at, :] = tn(x, dgate_ref[...]).astype(BF16)
        gu_ref[0, at, :] = tn(x, dup_ref[...]).astype(BF16)
        gd_ref[0, :, at] = tn(hidden_ref[...], columns(g_ref, at)).astype(BF16)
        return 0

    lax.fori_loop(0, 8, step, 0)


def grads(x_rows, g_rows, hidden, dgate, dup):
    rows, ff = hidden.shape
    width = 8 * x_rows.shape[2]
    return pl.pallas_call(
        grads_kernel,
        out_shape=[
            jax.ShapeDtypeStruct((1, width, ff), BF16),
            jax.ShapeDtypeStruct((1, width, ff), BF16),
            jax.ShapeDtypeStruct((1, ff, width), BF16),
        ],
        compiler_params=params(),
        cost_estimate=pl.CostEstimate(
            flops=6 * rows * 2048 * ff, bytes_accessed=10 * 2**20, transcendentals=0
        ),
        name="grads",
    )(x_rows, g_rows, hidden, dgate, dup)


def add_rows(place, scale, back):
    hot = one_hot(place)
    rows = jnp.concatenate(
        [back[2 * l].astype(F32) + back[2 * l + 1].astype(F32) for l in range(16)], axis=0
    )
    if scale is not None:
        rows = rows * row_weights(hot, scale)
    hi = rows.astype(BF16)
    low = (rows - hi.astype(F32)).astype(BF16)
    pick = as_bf16(hot)
    return tn(pick, hi) + tn(pick, low)


def join_out_kernel(z_ref, place_ref, weight_ref, back_ref, own_ref, *sum_refs):
    for shift, sum_ref in enumerate((own_ref, *sum_refs)):
        block = lax.rem(z_ref[0] + shift, 8)
        rows = back_ref.at[:, pl.ds(pl.multiple_of(block * CAP, CAP), CAP), :]
        sum_ref[...] = add_rows(place_ref[block], weight_ref[block], rows).astype(sum_ref.dtype)


def join_out(zs, place, weight, back):
    ntok, cut = place.shape[2], back.shape[2]
    shapes = [jax.ShapeDtypeStruct((ntok, cut), F32 if s == 0 else BF16) for s in range(8)]
    return pl.pallas_call(
        join_out_kernel,
        grid_spec=pltpu.PrefetchScalarGridSpec(
            num_scalar_prefetch=1,
            grid=(1,),
            in_specs=[whole(place.shape), whole(weight.shape), whole(back.shape)],
            out_specs=[whole((ntok, cut))] * 8,
        ),
        out_shape=shapes,
        compiler_params=params(),
        name="join_out",
    )(zs, place, weight, back)


def join_in_kernel(place_ref, back_ref, sum_ref):
    eighth = sum_ref.shape[0] // place_ref.shape[0]
    for b in range(place_ref.shape[0]):
        total = add_rows(place_ref[b], None, back_ref.at[:, b * CAP : (b + 1) * CAP, :])
        sum_ref[b * eighth : (b + 1) * eighth] = total.astype(BF16).reshape(eighth, *sum_ref.shape[1:])


def join_in(place, back):
    blocks, _, ntok = place.shape
    return pl.pallas_call(
        join_in_kernel,
        out_shape=jax.ShapeDtypeStruct((blocks * 8, ntok // 8, back.shape[2]), BF16),
        compiler_params=params(),
        name="join_in",
    )(place, back)


def total_kernel(col_ref, *refs):
    parts, pieces, total_ref = refs[:8], refs[8:16], refs[16]
    total = parts[0][...]
    for part in parts[1:]:
        total = total + part[...].astype(F32)
    total_ref[...] = total
    count = pieces[0].shape[0]
    for shift, piece in enumerate(pieces):
        to = lax.rem(col_ref[0] + shift, 8)
        piece[...] = total_ref[pl.ds(pl.multiple_of(to * count, count), count), :].astype(BF16)


def total(col, parts):
    ntok, cut = parts[0].shape
    return pl.pallas_call(
        total_kernel,
        grid_spec=pltpu.PrefetchScalarGridSpec(
            num_scalar_prefetch=1,
            grid=(1,),
            in_specs=[whole((ntok, cut))] * 8,
            out_specs=[whole((ntok // 8, cut))] * 8,
            scratch_shapes=[pltpu.VMEM((ntok, cut), F32)],
        ),
        out_shape=[jax.ShapeDtypeStruct((ntok // 8, cut), BF16)] * 8,
        compiler_params=params(),
        name="total",
    )(col, *parts)


def last_kernel(col_ref, *refs):
    pieces, part_ref, out_ref, in_ref = refs[:8], refs[8], refs[9], refs[10]
    cut = part_ref.shape[2]
    for shift, piece in enumerate(pieces):
        at = lax.rem(col_ref[0] + 8 - shift, 8) * cut
        out_ref[:, pl.ds(pl.multiple_of(at, cut), cut)] = piece[...]
    for e in range(8):
        whole_sum = part_ref[e].astype(F32)
        for z in range(1, 8):
            whole_sum = whole_sum + part_ref[z * 8 + e].astype(F32)
        in_ref[:, e * cut : (e + 1) * cut] = whole_sum.astype(BF16)


def last(col, pieces, parts):
    _, count, cut = parts.shape
    shape = jax.ShapeDtypeStruct((count, 8 * cut), BF16)
    return pl.pallas_call(
        last_kernel,
        grid_spec=pltpu.PrefetchScalarGridSpec(
            num_scalar_prefetch=1,
            grid=(1,),
            in_specs=[whole((count, cut))] * 8 + [whole(parts.shape)],
            out_specs=[whole(shape.shape)] * 2,
        ),
        out_shape=[shape, shape],
        compiler_params=params(),
        name="last",
    )(col, *pieces, parts)


def swap(buffer, axes):
    return lax.all_to_all(buffer, axes, split_axis=0, concat_axis=0, tiled=True)


def spread(arrays, axes):
    return [arrays[0]] + [
        lax.ppermute(arrays[shift], axes, [(i, (i + shift) % 8) for i in range(8)])
        for shift in range(1, 8)
    ]


def in_hbm(array):
    return pltpu.with_memory_space_constraint(array, pltpu.HBM)


def after(value, others):
    return lax.optimization_barrier((value, others))[0]


def cross(arrays):
    return [arrays[0]] + [
        lax.ppermute(
            array, ("xl", "core", "xh"), [(i, i ^ (2 * away + over)) for i in range(8)]
        )
        for (away, over), array in zip(ROUTES[1:], arrays[1:])
    ]


def on_device(
    tokens, expert_ids, route_weight, expert_slot, gate_weight, up_weight, down_weight, cotangent
):
    col = lax.axis_index(EX).astype(jnp.int32).reshape(1)
    zs = lax.axis_index("z").astype(jnp.int32).reshape(1)
    at = jnp.concatenate([zs, lax.axis_index(("xl", "core")).astype(jnp.int32).reshape(1), col])
    rw_t = route_weight.T
    x_cut, slots = route(col, tokens, expert_ids.T, rw_t, expert_slot.reshape(1, -1))
    x_all = swap(x_cut, ("z",))
    gate_weight, up_weight, down_weight = map(in_hbm, (gate_weight, up_weight, down_weight))
    g_crossed = [in_hbm(rows) for rows in cross(pick_g(at, cotangent, slots, rw_t))]
    x_all = after(x_all, g_crossed)
    g_turned = turn_g(at, g_crossed)
    g_parts = [in_hbm(part) for part in spread(g_turned, ("z",))]
    x_send, place, weight = pick_x(zs, x_all)
    x_rows = after(swap(x_send, PLANE), g_turned)
    out_send, gate, up, hidden = forward(x_rows, gate_weight, up_weight, down_weight)
    out_send = after(out_send, [g_parts[s] for s in EARLY])
    out_back = in_hbm(swap(out_send, PLANE))
    g_rows, in_send, dgate, dup = backward(
        at, g_parts, gate, up, gate_weight, up_weight, down_weight
    )
    in_back = swap(in_send, PLANE)
    weight_grads = grads(x_rows, g_rows, hidden, dgate, dup)
    y_parts = spread(join_out(zs, place, weight, out_back), ("z",))
    y_parts[0] = after(y_parts[0], weight_grads)
    pieces = total(col, y_parts)
    in_back, pieces = lax.optimization_barrier((in_back, pieces))
    dx_part = join_in(place, in_back)
    pieces = spread(pieces, EX)
    layer_out, input_grad = last(col, pieces, swap(dx_part, ("z", "xh", "y")))
    return layer_out, input_grad, *weight_grads


def solution(mesh):
    fine = Mesh(mesh.devices.reshape(8, 2, 2, 2, 4), ("z", "xl", "core", "xh", "y"))
    rows, every = P(DP, None), P(DP + EX, None)
    half = P(DP + EX, None, None)
    return jax.shard_map(
        on_device,
        mesh=fine,
        in_specs=(rows, rows, rows, P(), half, half, half, rows),
        out_specs=(every, every, half, half, half),
        check_vma=False,
    )
```

```python
import jax
import jax.numpy as jnp
from jax import lax
from jax.experimental import pallas as pl
from jax.experimental.pallas import tpu as pltpu
from jax.sharding import Mesh, PartitionSpec as P

DP = ("z", "xl", "core")
EX = ("xh", "y")
PLANE = ("xl", "core", "xh", "y")
BF16 = jnp.bfloat16
F32 = jnp.float32
CAP = 16
EARLY = (1, 2, 4, 6, 7)
META = 16


def nn(a, b):
    return lax.dot_general(a, b, (((1,), (0,)), ((), ())), preferred_element_type=F32)


def nt(a, b):
    return lax.dot_general(a, b, (((1,), (1,)), ((), ())), preferred_element_type=F32)


def tn(a, b):
    return lax.dot_general(a, b, (((0,), (0,)), ((), ())), preferred_element_type=F32)


def params(mib=16):
    return pltpu.CompilerParams(vmem_limit_bytes=mib * 2**20)


def whole(shape):
    return pl.BlockSpec(shape, lambda *_: (0,) * len(shape))


def route_kernel(col_ref, tok_ref, ids_ref, rw_ref, slot_ref, x_ref, slots_ref):
    ntok = tok_ref.shape[0]
    table = jnp.broadcast_to(slot_ref[...], (8, slot_ref.shape[1]))
    slots = jnp.take_along_axis(table, ids_ref[...], axis=1, mode="promise_in_bounds").astype(F32)
    slots_ref[...] = slots
    w = rw_ref[...]
    hi = w.astype(BF16).astype(F32)
    rest = w - hi
    mid = rest.astype(BF16).astype(F32)
    low = rest - mid
    tok = tok_ref[...]
    left = jnp.concatenate([slots, mid], axis=0).astype(BF16)
    right = jnp.concatenate([hi, low], axis=0).astype(BF16)
    for z in range(x_ref.shape[0]):
        x_ref[z, 0:ntok, :] = tok
        x_ref[z, ntok : ntok + META, 0:128] = left
        x_ref[z, ntok : ntok + META, 128:256] = right


def route(col, tokens, ids_t, rw_t, slot_row):
    ntok, width = tokens.shape
    cut = width // 8
    return pl.pallas_call(
        route_kernel,
        grid_spec=pltpu.PrefetchScalarGridSpec(
            num_scalar_prefetch=1,
            grid=(1,),
            in_specs=[
                pl.BlockSpec((ntok, cut), lambda i, c: (0, c[0])),
                whole(ids_t.shape),
                whole(rw_t.shape),
                whole(slot_row.shape),
            ],
            out_specs=[whole((8, ntok + META, cut)), whole(ids_t.shape)],
        ),
        out_shape=[
            jax.ShapeDtypeStruct((8, ntok + META, cut), BF16),
            jax.ShapeDtypeStruct(ids_t.shape, F32),
        ],
        compiler_params=params(60),
        name="route",
    )(col, tokens, ids_t, rw_t, slot_row)


def one_hot(place):
    slots, ntok = place.shape
    spread = jnp.broadcast_to(place[:, None, :], (slots, CAP, ntok)).reshape(slots * CAP, ntok)
    at = lax.broadcasted_iota(jnp.int32, (slots * CAP, ntok), 0) % CAP
    return spread == at.astype(F32)


def row_weights(hot, weight):
    slots, ntok = weight.shape
    spread = jnp.broadcast_to(weight[:, None, :], (slots, CAP, ntok)).reshape(slots * CAP, ntok)
    return jnp.sum(jnp.where(hot, spread, 0.0), axis=1, keepdims=True)


def as_bf16(hot):
    return jnp.where(hot, 1.0, 0.0).astype(BF16)


def put_rows(rows, send_ref):
    for l in range(rows.shape[0] // CAP):
        part = rows[l * CAP : (l + 1) * CAP]
        send_ref[2 * l] = part
        send_ref[2 * l + 1] = part


def places(slots, w, local, earlier):
    chosen = jnp.zeros(local.shape, F32)
    weight = jnp.zeros(local.shape, F32)
    for k in range(8):
        same = local == slots[k : k + 1, :]
        chosen = jnp.where(same, 1.0, chosen)
        weight = jnp.where(same, w[k : k + 1, :], weight)
    before = nn(chosen.astype(BF16), earlier)
    return jnp.where(chosen > 0.0, before, -1.0), weight


def earlier_tokens(ntok):
    row = lax.broadcasted_iota(jnp.int32, (ntok, ntok), 0)
    column = lax.broadcasted_iota(jnp.int32, (ntok, ntok), 1)
    return jnp.where(row < column, 1.0, 0.0).astype(BF16)


def pick_x_kernel(at_ref, x_ref, send_ref, place_ref, weight_ref):
    ntok = x_ref.shape[1] - META
    first = (at_ref[0] * 16).astype(F32)
    local = lax.broadcasted_iota(jnp.int32, (16, ntok), 0).astype(F32) + first
    earlier = earlier_tokens(ntok)
    for b in range(x_ref.shape[0]):
        left = x_ref[b, ntok : ntok + META, 0:128].astype(F32)
        right = x_ref[b, ntok : ntok + META, 128:256].astype(F32)
        w = right[0:8] + left[8:16] + right[8:16]
        place, weight = places(left[0:8], w, local, earlier)
        place_ref[b] = place
        weight_ref[b] = weight
        rows = nn(as_bf16(one_hot(place)), x_ref[b, 0:ntok, :])
        put_rows(rows.astype(BF16), send_ref.at[:, b * CAP : (b + 1) * CAP, :])


def pick_x(zs, x_all):
    blocks, rows, cut = x_all.shape
    ntok = rows - META
    return pl.pallas_call(
        pick_x_kernel,
        grid_spec=pltpu.PrefetchScalarGridSpec(
            num_scalar_prefetch=1,
            grid=(1,),
            in_specs=[whole(x_all.shape)],
            out_specs=[
                whole((32, blocks * CAP, cut)),
                whole((blocks, 16, ntok)),
                whole((blocks, 16, ntok)),
            ],
        ),
        out_shape=[
            pltpu.HBM((32, blocks * CAP, cut), BF16),
            jax.ShapeDtypeStruct((blocks, 16, ntok), F32),
            jax.ShapeDtypeStruct((blocks, 16, ntok), F32),
        ],
        compiler_params=params(),
        name="pick_x",
    )(zs, x_all)


ROUTES = ((0, 0), (1, 0), (2, 0), (2, 1), (3, 0), (3, 1))


def pick_g_kernel(at_ref, cot_ref, slots_ref, rw_ref, *send_refs):
    ntok, width = cot_ref.shape
    earlier = earlier_tokens(ntok)
    planes = lax.broadcasted_iota(jnp.int32, (8, ntok), 0)
    for (away, over), send_ref in zip(ROUTES, send_refs):
        local = planes * 16 + ((at_ref[1] ^ away) * 4 + ((at_ref[2] // 2) ^ (2 * over)))
        place, weight = places(slots_ref[...], rw_ref[...], local.astype(F32), earlier)
        hot = one_hot(place)
        pick, scale = as_bf16(hot), row_weights(hot, weight)
        begin = over * (width // 2)
        for c in range(0, send_ref.shape[1], 512):
            rows = nn(pick, cot_ref[:, begin + c : begin + c + 512]) * scale
            send_ref[:, c : c + 512] = rows.astype(BF16)


def pick_g(at, cotangent, slots, rw_t):
    ntok, width = cotangent.shape
    shapes = [(8 * CAP, width if away < 2 else width // 2) for away, _ in ROUTES]
    return pl.pallas_call(
        pick_g_kernel,
        grid_spec=pltpu.PrefetchScalarGridSpec(
            num_scalar_prefetch=1,
            grid=(1,),
            in_specs=[whole(cotangent.shape), whole(slots.shape), whole(rw_t.shape)],
            out_specs=[whole(shape) for shape in shapes],
        ),
        out_shape=[jax.ShapeDtypeStruct(shape, BF16) for shape in shapes],
        compiler_params=params(),
        name="pick_g",
    )(at, cotangent, slots, rw_t)


def turn_g_kernel(at_ref, *refs):
    given, send_refs = refs[: len(ROUTES)], refs[len(ROUTES) :]
    for shift, send_ref in enumerate(send_refs):
        to = pl.ds(pl.multiple_of(lax.rem(at_ref[0] + shift, 8) * CAP, CAP), CAP)
        for (away, over), rows in zip(ROUTES, given):
            begin, count = over * (send_ref.shape[1] // 2), rows.shape[1]
            send_ref[away * CAP : (away + 1) * CAP, begin : begin + count] = rows[to, :]


def turn_g(at, given):
    width = given[0].shape[1]
    return pl.pallas_call(
        turn_g_kernel,
        grid_spec=pltpu.PrefetchScalarGridSpec(
            num_scalar_prefetch=1,
            grid=(1,),
            in_specs=[whole(a.shape) for a in given],
            out_specs=[whole((4 * CAP, width))] * 8,
        ),
        out_shape=[pltpu.HBM((4 * CAP, width), BF16)] * 8,
        compiler_params=params(),
        name="turn_g",
    )(at, *given)


def chunk(ref, e):
    return jnp.concatenate([ref[q * 8 + e] for q in range(4)], axis=0)


def columns(ref, at):
    return jnp.concatenate([ref[q, :, at] for q in range(4)], axis=0)


def put_chunk(ref, e, rows):
    for q in range(4):
        ref[q * 8 + e] = rows[q * 128 : (q + 1) * 128]


def forward_kernel(x_ref, wg_ref, wu_ref, wd_ref, out_ref, gate_ref, up_ref, hidden_ref):
    cut = x_ref.shape[2]

    def first(e, _):
        at = pl.ds(pl.multiple_of(e * cut, cut), cut)
        x = chunk(x_ref, e)
        gate_ref[...] += nn(x, wg_ref[0, at, :])
        up_ref[...] += nn(x, wu_ref[0, at, :])
        return 0

    gate_ref[...] = jnp.zeros_like(gate_ref)
    up_ref[...] = jnp.zeros_like(up_ref)
    lax.fori_loop(0, 8, first, 0, unroll=8)
    gate = gate_ref[...]
    hidden_ref[...] = (gate * jax.nn.sigmoid(gate) * up_ref[...]).astype(BF16)

    def second(e, _):
        at = pl.ds(pl.multiple_of(e * cut, cut), cut)
        put_chunk(out_ref, e, nn(hidden_ref[...], wd_ref[0, :, at]).astype(BF16))
        return 0

    lax.fori_loop(0, 8, second, 0, unroll=8)


def forward(x_rows, wg, wu, wd):
    rows, ff = 512, wg.shape[2]
    return pl.pallas_call(
        forward_kernel,
        out_shape=[
            pltpu.HBM(x_rows.shape, BF16),
            pltpu.HBM((rows, ff), F32),
            pltpu.HBM((rows, ff), F32),
            pltpu.HBM((rows, ff), BF16),
        ],
        compiler_params=params(),
        cost_estimate=pl.CostEstimate(
            flops=6 * rows * 2048 * ff, bytes_accessed=11 * 2**20, transcendentals=rows * ff
        ),
        name="forward",
    )(x_rows, wg, wu, wd)


def backward_kernel(at_ref, *refs):
    parts, (gate_ref, up_ref, wg_ref, wu_ref, wd_ref) = refs[:8], refs[8:13]
    g_ref, in_ref, dgate_ref, dup_ref, back_ref = refs[13:]
    cut = in_ref.shape[2]
    for shift, part in enumerate(parts):
        rows = pl.ds(pl.multiple_of(lax.rem(at_ref[0] + 8 - shift, 8) * CAP, CAP), CAP)
        for away in range(4):
            g_ref[at_ref[1] ^ away, rows, :] = part[away * CAP : (away + 1) * CAP, :]

    def first(e, _):
        at = pl.ds(pl.multiple_of(e * cut, cut), cut)
        back_ref[...] += nt(columns(g_ref, at), wd_ref[0, :, at])
        return 0

    back_ref[...] = jnp.zeros_like(back_ref)
    lax.fori_loop(0, 8, first, 0, unroll=8)
    back, gate = back_ref[...], gate_ref[...]
    sigma = jax.nn.sigmoid(gate)
    dgate_ref[...] = (back * up_ref[...] * sigma * (1.0 + gate * (1.0 - sigma))).astype(BF16)
    dup_ref[...] = (back * (gate * sigma)).astype(BF16)

    def second(e, _):
        at = pl.ds(pl.multiple_of(e * cut, cut), cut)
        piece = nt(dgate_ref[...], wg_ref[0, at, :]) + nt(dup_ref[...], wu_ref[0, at, :])
        put_chunk(in_ref, e, piece.astype(BF16))
        return 0

    lax.fori_loop(0, 8, second, 0, unroll=8)


def backward(at, parts, gate, up, wg, wu, wd):
    rows, ff = gate.shape
    width = wd.shape[2]
    return pl.pallas_call(
        backward_kernel,
        grid_spec=pltpu.PrefetchScalarGridSpec(
            num_scalar_prefetch=1,
            grid=(1,),
            in_specs=[whole(a.shape) for a in (*parts, gate, up, wg, wu, wd)],
            out_specs=[
                whole((4, rows // 4, width)),
                whole((32, rows // 4, width // 8)),
                whole((rows, ff)),
                whole((rows, ff)),
            ],
            scratch_shapes=[pltpu.VMEM((rows, ff), F32)],
        ),
        out_shape=[
            pltpu.HBM((4, rows // 4, width), BF16),
            pltpu.HBM((32, rows // 4, width // 8), BF16),
            pltpu.HBM((rows, ff), BF16),
            pltpu.HBM((rows, ff), BF16),
        ],
        compiler_params=params(36),
        cost_estimate=pl.CostEstimate(
            flops=6 * rows * 2048 * ff, bytes_accessed=13 * 2**20, transcendentals=rows * ff
        ),
        name="backward",
    )(at, *parts, gate, up, wg, wu, wd)


def grads_kernel(x_ref, g_ref, hidden_ref, dgate_ref, dup_ref, gg_ref, gu_ref, gd_ref):
    cut = x_ref.shape[2]

    def step(e, _):
        at = pl.ds(pl.multiple_of(e * cut, cut), cut)
        x = chunk(x_ref, e)
        gg_ref[0, at, :] = tn(x, dgate_ref[...]).astype(BF16)
        gu_ref[0, at, :] = tn(x, dup_ref[...]).astype(BF16)
        gd_ref[0, :, at] = tn(hidden_ref[...], columns(g_ref, at)).astype(BF16)
        return 0

    lax.fori_loop(0, 8, step, 0)


def grads(x_rows, g_rows, hidden, dgate, dup):
    rows, ff = hidden.shape
    width = 8 * x_rows.shape[2]
    return pl.pallas_call(
        grads_kernel,
        out_shape=[
            jax.ShapeDtypeStruct((1, width, ff), BF16),
            jax.ShapeDtypeStruct((1, width, ff), BF16),
            jax.ShapeDtypeStruct((1, ff, width), BF16),
        ],
        compiler_params=params(),
        cost_estimate=pl.CostEstimate(
            flops=6 * rows * 2048 * ff, bytes_accessed=10 * 2**20, transcendentals=0
        ),
        name="grads",
    )(x_rows, g_rows, hidden, dgate, dup)


def add_rows(place, scale, back):
    hot = one_hot(place)
    rows = jnp.concatenate(
        [back[2 * l].astype(F32) + back[2 * l + 1].astype(F32) for l in range(16)], axis=0
    )
    if scale is not None:
        rows = rows * row_weights(hot, scale)
    hi = rows.astype(BF16)
    low = (rows - hi.astype(F32)).astype(BF16)
    pick = as_bf16(hot)
    return tn(pick, hi) + tn(pick, low)


def join_out_kernel(z_ref, place_ref, weight_ref, back_ref, own_ref, *sum_refs):
    for shift, sum_ref in enumerate((own_ref, *sum_refs)):
        block = lax.rem(z_ref[0] + shift, 8)
        rows = back_ref.at[:, pl.ds(pl.multiple_of(block * CAP, CAP), CAP), :]
        sum_ref[...] = add_rows(place_ref[block], weight_ref[block], rows).astype(sum_ref.dtype)


def join_out(zs, place, weight, back):
    ntok, cut = place.shape[2], back.shape[2]
    shapes = [jax.ShapeDtypeStruct((ntok, cut), F32 if s == 0 else BF16) for s in range(8)]
    return pl.pallas_call(
        join_out_kernel,
        grid_spec=pltpu.PrefetchScalarGridSpec(
            num_scalar_prefetch=1,
            grid=(1,),
            in_specs=[whole(place.shape), whole(weight.shape), whole(back.shape)],
            out_specs=[whole((ntok, cut))] * 8,
        ),
        out_shape=shapes,
        compiler_params=params(),
        name="join_out",
    )(zs, place, weight, back)


def join_in_kernel(place_ref, back_ref, sum_ref):
    eighth = sum_ref.shape[0] // place_ref.shape[0]
    for b in range(place_ref.shape[0]):
        total = add_rows(place_ref[b], None, back_ref.at[:, b * CAP : (b + 1) * CAP, :])
        sum_ref[b * eighth : (b + 1) * eighth] = total.astype(BF16).reshape(eighth, *sum_ref.shape[1:])


def join_in(place, back):
    blocks, _, ntok = place.shape
    return pl.pallas_call(
        join_in_kernel,
        out_shape=jax.ShapeDtypeStruct((blocks * 8, ntok // 8, back.shape[2]), BF16),
        compiler_params=params(),
        name="join_in",
    )(place, back)


def total_kernel(col_ref, *refs):
    parts, pieces, total_ref = refs[:8], refs[8:16], refs[16]
    total = parts[0][...]
    for part in parts[1:]:
        total = total + part[...].astype(F32)
    total_ref[...] = total
    count = pieces[0].shape[0]
    for shift, piece in enumerate(pieces):
        to = lax.rem(col_ref[0] + shift, 8)
        piece[...] = total_ref[pl.ds(pl.multiple_of(to * count, count), count), :].astype(BF16)


def total(col, parts):
    ntok, cut = parts[0].shape
    return pl.pallas_call(
        total_kernel,
        grid_spec=pltpu.PrefetchScalarGridSpec(
            num_scalar_prefetch=1,
            grid=(1,),
            in_specs=[whole((ntok, cut))] * 8,
            out_specs=[whole((ntok // 8, cut))] * 8,
            scratch_shapes=[pltpu.VMEM((ntok, cut), F32)],
        ),
        out_shape=[jax.ShapeDtypeStruct((ntok // 8, cut), BF16)] * 8,
        compiler_params=params(),
        name="total",
    )(col, *parts)


def last_kernel(col_ref, *refs):
    pieces, part_ref, out_ref, in_ref = refs[:8], refs[8], refs[9], refs[10]
    cut = part_ref.shape[2]
    for shift, piece in enumerate(pieces):
        at = lax.rem(col_ref[0] + 8 - shift, 8) * cut
        out_ref[:, pl.ds(pl.multiple_of(at, cut), cut)] = piece[...]
    for e in range(8):
        whole_sum = part_ref[e].astype(F32)
        for z in range(1, 8):
            whole_sum = whole_sum + part_ref[z * 8 + e].astype(F32)
        in_ref[:, e * cut : (e + 1) * cut] = whole_sum.astype(BF16)


def last(col, pieces, parts):
    _, count, cut = parts.shape
    shape = jax.ShapeDtypeStruct((count, 8 * cut), BF16)
    return pl.pallas_call(
        last_kernel,
        grid_spec=pltpu.PrefetchScalarGridSpec(
            num_scalar_prefetch=1,
            grid=(1,),
            in_specs=[whole((count, cut))] * 8 + [whole(parts.shape)],
            out_specs=[whole(shape.shape)] * 2,
        ),
        out_shape=[shape, shape],
        compiler_params=params(),
        name="last",
    )(col, *pieces, parts)


def swap(buffer, axes):
    return lax.all_to_all(buffer, axes, split_axis=0, concat_axis=0, tiled=True)


def spread(arrays, axes):
    return [arrays[0]] + [
        lax.ppermute(arrays[shift], axes, [(i, (i + shift) % 8) for i in range(8)])
        for shift in range(1, 8)
    ]


def in_hbm(array):
    return pltpu.with_memory_space_constraint(array, pltpu.HBM)


def after(value, others):
    return lax.optimization_barrier((value, others))[0]


def cross(arrays):
    return [arrays[0]] + [
        lax.ppermute(
            array, ("xl", "core", "xh"), [(i, i ^ (2 * away + over)) for i in range(8)]
        )
        for (away, over), array in zip(ROUTES[1:], arrays[1:])
    ]


def on_device(
    tokens, expert_ids, route_weight, expert_slot, gate_weight, up_weight, down_weight, cotangent
):
    col = lax.axis_index(EX).astype(jnp.int32).reshape(1)
    zs = lax.axis_index("z").astype(jnp.int32).reshape(1)
    at = jnp.concatenate([zs, lax.axis_index(("xl", "core")).astype(jnp.int32).reshape(1), col])
    rw_t = route_weight.T
    x_cut, slots = route(col, tokens, expert_ids.T, rw_t, expert_slot.reshape(1, -1))
    x_all = swap(x_cut, ("z",))
    gate_weight, up_weight, down_weight = map(in_hbm, (gate_weight, up_weight, down_weight))
    g_crossed = [in_hbm(rows) for rows in cross(pick_g(at, cotangent, slots, rw_t))]
    x_all = after(x_all, g_crossed)
    g_turned = turn_g(at, g_crossed)
    g_parts = [in_hbm(part) for part in spread(g_turned, ("z",))]
    x_send, place, weight = pick_x(zs, x_all)
    x_rows = after(swap(x_send, PLANE), g_turned)
    out_send, gate, up, hidden = forward(x_rows, gate_weight, up_weight, down_weight)
    out_send = after(out_send, [g_parts[s] for s in EARLY])
    out_back = in_hbm(swap(out_send, PLANE))
    g_rows, in_send, dgate, dup = backward(
        at, g_parts, gate, up, gate_weight, up_weight, down_weight
    )
    in_back = swap(in_send, PLANE)
    weight_grads = grads(x_rows, g_rows, hidden, dgate, dup)
    y_parts = spread(join_out(zs, place, weight, out_back), ("z",))
    y_parts[0] = after(y_parts[0], weight_grads)
    pieces = total(col, y_parts)
    in_back, pieces = lax.optimization_barrier((in_back, pieces))
    dx_part = join_in(place, in_back)
    pieces = spread(pieces, EX)
    layer_out, input_grad = last(col, pieces, swap(dx_part, ("z", "xh", "y")))
    return layer_out, input_grad, *weight_grads


def solution(mesh):
    fine = Mesh(mesh.devices.reshape(8, 2, 2, 2, 4), ("z", "xl", "core", "xh", "y"))
    rows, every = P(DP, None), P(DP + EX, None)
    half = P(DP + EX, None, None)
    return jax.shard_map(
        on_device,
        mesh=fine,
        in_specs=(rows, rows, rows, P(), half, half, half, rows),
        out_specs=(every, every, half, half, half),
        check_vma=False,
    )
```

```python
import jax
import jax.numpy as jnp
from jax import lax
from jax.experimental import pallas as pl
from jax.experimental.pallas import tpu as pltpu
from jax.sharding import Mesh, PartitionSpec as P

DP = ("z", "xl", "core")
EX = ("xh", "y")
PLANE = ("xl", "core", "xh", "y")
BF16 = jnp.bfloat16
F32 = jnp.float32
CAP = 16
EARLY = (1, 2, 4, 6, 7)
META = 16


def nn(a, b):
    return lax.dot_general(a, b, (((1,), (0,)), ((), ())), preferred_element_type=F32)


def nt(a, b):
    return lax.dot_general(a, b, (((1,), (1,)), ((), ())), preferred_element_type=F32)


def tn(a, b):
    return lax.dot_general(a, b, (((0,), (0,)), ((), ())), preferred_element_type=F32)


def params(mib=16):
    return pltpu.CompilerParams(vmem_limit_bytes=mib * 2**20)


def whole(shape):
    return pl.BlockSpec(shape, lambda *_: (0,) * len(shape))


def route_kernel(col_ref, tok_ref, ids_ref, rw_ref, slot_ref, x_ref, slots_ref):
    ntok = tok_ref.shape[0]
    table = jnp.broadcast_to(slot_ref[...], (8, slot_ref.shape[1]))
    slots = jnp.take_along_axis(table, ids_ref[...], axis=1, mode="promise_in_bounds").astype(F32)
    slots_ref[...] = slots
    w = rw_ref[...]
    hi = w.astype(BF16).astype(F32)
    rest = w - hi
    mid = rest.astype(BF16).astype(F32)
    low = rest - mid
    tok = tok_ref[...]
    left = jnp.concatenate([slots, mid], axis=0).astype(BF16)
    right = jnp.concatenate([hi, low], axis=0).astype(BF16)
    for z in range(x_ref.shape[0]):
        x_ref[z, 0:ntok, :] = tok
        x_ref[z, ntok : ntok + META, 0:128] = left
        x_ref[z, ntok : ntok + META, 128:256] = right


def route(col, tokens, ids_t, rw_t, slot_row):
    ntok, width = tokens.shape
    cut = width // 8
    return pl.pallas_call(
        route_kernel,
        grid_spec=pltpu.PrefetchScalarGridSpec(
            num_scalar_prefetch=1,
            grid=(1,),
            in_specs=[
                pl.BlockSpec((ntok, cut), lambda i, c: (0, c[0])),
                whole(ids_t.shape),
                whole(rw_t.shape),
                whole(slot_row.shape),
            ],
            out_specs=[whole((8, ntok + META, cut)), whole(ids_t.shape)],
        ),
        out_shape=[
            jax.ShapeDtypeStruct((8, ntok + META, cut), BF16),
            jax.ShapeDtypeStruct(ids_t.shape, F32),
        ],
        compiler_params=params(60),
        name="route",
    )(col, tokens, ids_t, rw_t, slot_row)


def one_hot(place):
    slots, ntok = place.shape
    spread = jnp.broadcast_to(place[:, None, :], (slots, CAP, ntok)).reshape(slots * CAP, ntok)
    at = lax.broadcasted_iota(jnp.int32, (slots * CAP, ntok), 0) % CAP
    return spread == at.astype(F32)


def row_weights(hot, weight):
    slots, ntok = weight.shape
    spread = jnp.broadcast_to(weight[:, None, :], (slots, CAP, ntok)).reshape(slots * CAP, ntok)
    return jnp.sum(jnp.where(hot, spread, 0.0), axis=1, keepdims=True)


def as_bf16(hot):
    return jnp.where(hot, 1.0, 0.0).astype(BF16)


def put_rows(rows, send_ref):
    for l in range(rows.shape[0] // CAP):
        part = rows[l * CAP : (l + 1) * CAP]
        send_ref[2 * l] = part
        send_ref[2 * l + 1] = part


def places(slots, w, local, earlier):
    chosen = jnp.zeros(local.shape, F32)
    weight = jnp.zeros(local.shape, F32)
    for k in range(8):
        same = local == slots[k : k + 1, :]
        chosen = jnp.where(same, 1.0, chosen)
        weight = jnp.where(same, w[k : k + 1, :], weight)
    before = nn(chosen.astype(BF16), earlier)
    return jnp.where(chosen > 0.0, before, -1.0), weight


def earlier_tokens(ntok):
    row = lax.broadcasted_iota(jnp.int32, (ntok, ntok), 0)
    column = lax.broadcasted_iota(jnp.int32, (ntok, ntok), 1)
    return jnp.where(row < column, 1.0, 0.0).astype(BF16)


def pick_x_kernel(at_ref, x_ref, send_ref, place_ref, weight_ref):
    ntok = x_ref.shape[1] - META
    first = (at_ref[0] * 16).astype(F32)
    local = lax.broadcasted_iota(jnp.int32, (16, ntok), 0).astype(F32) + first
    earlier = earlier_tokens(ntok)
    for b in range(x_ref.shape[0]):
        left = x_ref[b, ntok : ntok + META, 0:128].astype(F32)
        right = x_ref[b, ntok : ntok + META, 128:256].astype(F32)
        w = right[0:8] + left[8:16] + right[8:16]
        place, weight = places(left[0:8], w, local, earlier)
        place_ref[b] = place
        weight_ref[b] = weight
        rows = nn(as_bf16(one_hot(place)), x_ref[b, 0:ntok, :])
        put_rows(rows.astype(BF16), send_ref.at[:, b * CAP : (b + 1) * CAP, :])


def pick_x(zs, x_all):
    blocks, rows, cut = x_all.shape
    ntok = rows - META
    return pl.pallas_call(
        pick_x_kernel,
        grid_spec=pltpu.PrefetchScalarGridSpec(
            num_scalar_prefetch=1,
            grid=(1,),
            in_specs=[whole(x_all.shape)],
            out_specs=[
                whole((32, blocks * CAP, cut)),
                whole((blocks, 16, ntok)),
                whole((blocks, 16, ntok)),
            ],
        ),
        out_shape=[
            pltpu.HBM((32, blocks * CAP, cut), BF16),
            jax.ShapeDtypeStruct((blocks, 16, ntok), F32),
            jax.ShapeDtypeStruct((blocks, 16, ntok), F32),
        ],
        compiler_params=params(),
        name="pick_x",
    )(zs, x_all)


ROUTES = ((0, 0), (1, 0), (2, 0), (2, 1), (3, 0), (3, 1))


def pick_g_kernel(at_ref, cot_ref, slots_ref, rw_ref, *send_refs):
    ntok, width = cot_ref.shape
    earlier = earlier_tokens(ntok)
    planes = lax.broadcasted_iota(jnp.int32, (8, ntok), 0)
    for (away, over), send_ref in zip(ROUTES, send_refs):
        local = planes * 16 + ((at_ref[1] ^ away) * 4 + ((at_ref[2] // 2) ^ (2 * over)))
        place, weight = places(slots_ref[...], rw_ref[...], local.astype(F32), earlier)
        hot = one_hot(place)
        pick, scale = as_bf16(hot), row_weights(hot, weight)
        begin = over * (width // 2)
        for c in range(0, send_ref.shape[1], 512):
            rows = nn(pick, cot_ref[:, begin + c : begin + c + 512]) * scale
            send_ref[:, c : c + 512] = rows.astype(BF16)


def pick_g(at, cotangent, slots, rw_t):
    ntok, width = cotangent.shape
    shapes = [(8 * CAP, width if away < 2 else width // 2) for away, _ in ROUTES]
    return pl.pallas_call(
        pick_g_kernel,
        grid_spec=pltpu.PrefetchScalarGridSpec(
            num_scalar_prefetch=1,
            grid=(1,),
            in_specs=[whole(cotangent.shape), whole(slots.shape), whole(rw_t.shape)],
            out_specs=[whole(shape) for shape in shapes],
        ),
        out_shape=[jax.ShapeDtypeStruct(shape, BF16) for shape in shapes],
        compiler_params=params(),
        name="pick_g",
    )(at, cotangent, slots, rw_t)


def turn_g_kernel(at_ref, *refs):
    given, send_refs = refs[: len(ROUTES)], refs[len(ROUTES) :]
    for shift, send_ref in enumerate(send_refs):
        to = pl.ds(pl.multiple_of(lax.rem(at_ref[0] + shift, 8) * CAP, CAP), CAP)
        for (away, over), rows in zip(ROUTES, given):
            begin, count = over * (send_ref.shape[1] // 2), rows.shape[1]
            send_ref[away * CAP : (away + 1) * CAP, begin : begin + count] = rows[to, :]


def turn_g(at, given):
    width = given[0].shape[1]
    return pl.pallas_call(
        turn_g_kernel,
        grid_spec=pltpu.PrefetchScalarGridSpec(
            num_scalar_prefetch=1,
            grid=(1,),
            in_specs=[whole(a.shape) for a in given],
            out_specs=[whole((4 * CAP, width))] * 8,
        ),
        out_shape=[pltpu.HBM((4 * CAP, width), BF16)] * 8,
        compiler_params=params(),
        name="turn_g",
    )(at, *given)


def chunk(ref, e):
    return jnp.concatenate([ref[q * 8 + e] for q in range(4)], axis=0)


def columns(ref, at):
    return jnp.concatenate([ref[q, :, at] for q in range(4)], axis=0)


def put_chunk(ref, e, rows):
    for q in range(4):
        ref[q * 8 + e] = rows[q * 128 : (q + 1) * 128]


def forward_kernel(x_ref, wg_ref, wu_ref, wd_ref, out_ref, gate_ref, up_ref, hidden_ref):
    cut = x_ref.shape[2]

    def first(e, _):
        at = pl.ds(pl.multiple_of(e * cut, cut), cut)
        x = chunk(x_ref, e)
        gate_ref[...] += nn(x, wg_ref[0, at, :])
        up_ref[...] += nn(x, wu_ref[0, at, :])
        return 0

    gate_ref[...] = jnp.zeros_like(gate_ref)
    up_ref[...] = jnp.zeros_like(up_ref)
    lax.fori_loop(0, 8, first, 0, unroll=8)
    gate = gate_ref[...]
    hidden_ref[...] = (gate * jax.nn.sigmoid(gate) * up_ref[...]).astype(BF16)

    def second(e, _):
        at = pl.ds(pl.multiple_of(e * cut, cut), cut)
        put_chunk(out_ref, e, nn(hidden_ref[...], wd_ref[0, :, at]).astype(BF16))
        return 0

    lax.fori_loop(0, 8, second, 0, unroll=8)


def forward(x_rows, wg, wu, wd):
    rows, ff = 512, wg.shape[2]
    return pl.pallas_call(
        forward_kernel,
        out_shape=[
            pltpu.HBM(x_rows.shape, BF16),
            pltpu.HBM((rows, ff), F32),
            pltpu.HBM((rows, ff), F32),
            pltpu.HBM((rows, ff), BF16),
        ],
        compiler_params=params(),
        cost_estimate=pl.CostEstimate(
            flops=6 * rows * 2048 * ff, bytes_accessed=11 * 2**20, transcendentals=rows * ff
        ),
        name="forward",
    )(x_rows, wg, wu, wd)


def backward_kernel(at_ref, *refs):
    parts, (gate_ref, up_ref, wg_ref, wu_ref, wd_ref) = refs[:8], refs[8:13]
    g_ref, in_ref, dgate_ref, dup_ref, back_ref = refs[13:]
    cut = in_ref.shape[2]
    for shift, part in enumerate(parts):
        rows = pl.ds(pl.multiple_of(lax.rem(at_ref[0] + 8 - shift, 8) * CAP, CAP), CAP)
        for away in range(4):
            g_ref[at_ref[1] ^ away, rows, :] = part[away * CAP : (away + 1) * CAP, :]

    def first(e, _):
        at = pl.ds(pl.multiple_of(e * cut, cut), cut)
        back_ref[...] += nt(columns(g_ref, at), wd_ref[0, :, at])
        return 0

    back_ref[...] = jnp.zeros_like(back_ref)
    lax.fori_loop(0, 8, first, 0, unroll=8)
    back, gate = back_ref[...], gate_ref[...]
    sigma = jax.nn.sigmoid(gate)
    dgate_ref[...] = (back * up_ref[...] * sigma * (1.0 + gate * (1.0 - sigma))).astype(BF16)
    dup_ref[...] = (back * (gate * sigma)).astype(BF16)

    def second(e, _):
        at = pl.ds(pl.multiple_of(e * cut, cut), cut)
        piece = nt(dgate_ref[...], wg_ref[0, at, :]) + nt(dup_ref[...], wu_ref[0, at, :])
        put_chunk(in_ref, e, piece.astype(BF16))
        return 0

    lax.fori_loop(0, 8, second, 0, unroll=8)


def backward(at, parts, gate, up, wg, wu, wd):
    rows, ff = gate.shape
    width = wd.shape[2]
    return pl.pallas_call(
        backward_kernel,
        grid_spec=pltpu.PrefetchScalarGridSpec(
            num_scalar_prefetch=1,
            grid=(1,),
            in_specs=[whole(a.shape) for a in (*parts, gate, up, wg, wu, wd)],
            out_specs=[
                whole((4, rows // 4, width)),
                whole((32, rows // 4, width // 8)),
                whole((rows, ff)),
                whole((rows, ff)),
            ],
            scratch_shapes=[pltpu.VMEM((rows, ff), F32)],
        ),
        out_shape=[
            pltpu.HBM((4, rows // 4, width), BF16),
            pltpu.HBM((32, rows // 4, width // 8), BF16),
            pltpu.HBM((rows, ff), BF16),
            pltpu.HBM((rows, ff), BF16),
        ],
        compiler_params=params(36),
        cost_estimate=pl.CostEstimate(
            flops=6 * rows * 2048 * ff, bytes_accessed=13 * 2**20, transcendentals=rows * ff
        ),
        name="backward",
    )(at, *parts, gate, up, wg, wu, wd)


def grads_kernel(x_ref, g_ref, hidden_ref, dgate_ref, dup_ref, gg_ref, gu_ref, gd_ref):
    cut = x_ref.shape[2]

    def step(e, _):
        at = pl.ds(pl.multiple_of(e * cut, cut), cut)
        x = chunk(x_ref, e)
        gg_ref[0, at, :] = tn(x, dgate_ref[...]).astype(BF16)
        gu_ref[0, at, :] = tn(x, dup_ref[...]).astype(BF16)
        gd_ref[0, :, at] = tn(hidden_ref[...], columns(g_ref, at)).astype(BF16)
        return 0

    lax.fori_loop(0, 8, step, 0, unroll=8)


def grads(x_rows, g_rows, hidden, dgate, dup):
    rows, ff = hidden.shape
    width = 8 * x_rows.shape[2]
    return pl.pallas_call(
        grads_kernel,
        out_shape=[
            jax.ShapeDtypeStruct((1, width, ff), BF16),
            jax.ShapeDtypeStruct((1, width, ff), BF16),
            jax.ShapeDtypeStruct((1, ff, width), BF16),
        ],
        compiler_params=params(),
        cost_estimate=pl.CostEstimate(
            flops=6 * rows * 2048 * ff, bytes_accessed=10 * 2**20, transcendentals=0
        ),
        name="grads",
    )(x_rows, g_rows, hidden, dgate, dup)


def add_rows(place, scale, back):
    hot = one_hot(place)
    rows = jnp.concatenate(
        [back[2 * l].astype(F32) + back[2 * l + 1].astype(F32) for l in range(16)], axis=0
    )
    if scale is not None:
        rows = rows * row_weights(hot, scale)
    hi = rows.astype(BF16)
    low = (rows - hi.astype(F32)).astype(BF16)
    pick = as_bf16(hot)
    return tn(pick, hi) + tn(pick, low)


def join_out_kernel(z_ref, place_ref, weight_ref, back_ref, own_ref, *sum_refs):
    for shift, sum_ref in enumerate((own_ref, *sum_refs)):
        block = lax.rem(z_ref[0] + shift, 8)
        rows = back_ref.at[:, pl.ds(pl.multiple_of(block * CAP, CAP), CAP), :]
        sum_ref[...] = add_rows(place_ref[block], weight_ref[block], rows).astype(sum_ref.dtype)


def join_out(zs, place, weight, back):
    ntok, cut = place.shape[2], back.shape[2]
    shapes = [jax.ShapeDtypeStruct((ntok, cut), F32 if s == 0 else BF16) for s in range(8)]
    return pl.pallas_call(
        join_out_kernel,
        grid_spec=pltpu.PrefetchScalarGridSpec(
            num_scalar_prefetch=1,
            grid=(1,),
            in_specs=[whole(place.shape), whole(weight.shape), whole(back.shape)],
            out_specs=[whole((ntok, cut))] * 8,
        ),
        out_shape=shapes,
        compiler_params=params(),
        name="join_out",
    )(zs, place, weight, back)


def join_in_kernel(place_ref, back_ref, sum_ref):
    eighth = sum_ref.shape[0] // place_ref.shape[0]
    for b in range(place_ref.shape[0]):
        total = add_rows(place_ref[b], None, back_ref.at[:, b * CAP : (b + 1) * CAP, :])
        sum_ref[b * eighth : (b + 1) * eighth] = total.astype(BF16).reshape(eighth, *sum_ref.shape[1:])


def join_in(place, back):
    blocks, _, ntok = place.shape
    return pl.pallas_call(
        join_in_kernel,
        out_shape=jax.ShapeDtypeStruct((blocks * 8, ntok // 8, back.shape[2]), BF16),
        compiler_params=params(),
        name="join_in",
    )(place, back)


def total_kernel(col_ref, *refs):
    parts, pieces, total_ref = refs[:8], refs[8:16], refs[16]
    total = parts[0][...]
    for part in parts[1:]:
        total = total + part[...].astype(F32)
    total_ref[...] = total
    count = pieces[0].shape[0]
    for shift, piece in enumerate(pieces):
        to = lax.rem(col_ref[0] + shift, 8)
        piece[...] = total_ref[pl.ds(pl.multiple_of(to * count, count), count), :].astype(BF16)


def total(col, parts):
    ntok, cut = parts[0].shape
    return pl.pallas_call(
        total_kernel,
        grid_spec=pltpu.PrefetchScalarGridSpec(
            num_scalar_prefetch=1,
            grid=(1,),
            in_specs=[whole((ntok, cut))] * 8,
            out_specs=[whole((ntok // 8, cut))] * 8,
            scratch_shapes=[pltpu.VMEM((ntok, cut), F32)],
        ),
        out_shape=[jax.ShapeDtypeStruct((ntok // 8, cut), BF16)] * 8,
        compiler_params=params(),
        name="total",
    )(col, *parts)


def last_kernel(col_ref, *refs):
    pieces, part_ref, out_ref, in_ref = refs[:8], refs[8], refs[9], refs[10]
    cut = part_ref.shape[2]
    for shift, piece in enumerate(pieces):
        at = lax.rem(col_ref[0] + 8 - shift, 8) * cut
        out_ref[:, pl.ds(pl.multiple_of(at, cut), cut)] = piece[...]
    for e in range(8):
        whole_sum = part_ref[e].astype(F32)
        for z in range(1, 8):
            whole_sum = whole_sum + part_ref[z * 8 + e].astype(F32)
        in_ref[:, e * cut : (e + 1) * cut] = whole_sum.astype(BF16)


def last(col, pieces, parts):
    _, count, cut = parts.shape
    shape = jax.ShapeDtypeStruct((count, 8 * cut), BF16)
    return pl.pallas_call(
        last_kernel,
        grid_spec=pltpu.PrefetchScalarGridSpec(
            num_scalar_prefetch=1,
            grid=(1,),
            in_specs=[whole((count, cut))] * 8 + [whole(parts.shape)],
            out_specs=[whole(shape.shape)] * 2,
        ),
        out_shape=[shape, shape],
        compiler_params=params(),
        name="last",
    )(col, *pieces, parts)


def swap(buffer, axes):
    return lax.all_to_all(buffer, axes, split_axis=0, concat_axis=0, tiled=True)


def spread(arrays, axes):
    return [arrays[0]] + [
        lax.ppermute(arrays[shift], axes, [(i, (i + shift) % 8) for i in range(8)])
        for shift in range(1, 8)
    ]


def in_hbm(array):
    return pltpu.with_memory_space_constraint(array, pltpu.HBM)


def after(value, others):
    return lax.optimization_barrier((value, others))[0]


def cross(arrays):
    return [arrays[0]] + [
        lax.ppermute(
            array, ("xl", "core", "xh"), [(i, i ^ (2 * away + over)) for i in range(8)]
        )
        for (away, over), array in zip(ROUTES[1:], arrays[1:])
    ]


def on_device(
    tokens, expert_ids, route_weight, expert_slot, gate_weight, up_weight, down_weight, cotangent
):
    col = lax.axis_index(EX).astype(jnp.int32).reshape(1)
    zs = lax.axis_index("z").astype(jnp.int32).reshape(1)
    at = jnp.concatenate([zs, lax.axis_index(("xl", "core")).astype(jnp.int32).reshape(1), col])
    rw_t = route_weight.T
    x_cut, slots = route(col, tokens, expert_ids.T, rw_t, expert_slot.reshape(1, -1))
    x_all = swap(x_cut, ("z",))
    gate_weight, up_weight, down_weight = map(in_hbm, (gate_weight, up_weight, down_weight))
    g_crossed = [in_hbm(rows) for rows in cross(pick_g(at, cotangent, slots, rw_t))]
    x_all = after(x_all, g_crossed)
    g_turned = turn_g(at, g_crossed)
    g_parts = [in_hbm(part) for part in spread(g_turned, ("z",))]
    x_send, place, weight = pick_x(zs, x_all)
    x_rows = after(swap(x_send, PLANE), g_turned)
    out_send, gate, up, hidden = forward(x_rows, gate_weight, up_weight, down_weight)
    out_send = after(out_send, [g_parts[s] for s in EARLY])
    out_back = in_hbm(swap(out_send, PLANE))
    g_rows, in_send, dgate, dup = backward(
        at, g_parts, gate, up, gate_weight, up_weight, down_weight
    )
    in_back = swap(in_send, PLANE)
    weight_grads = grads(x_rows, g_rows, hidden, dgate, dup)
    y_parts = spread(join_out(zs, place, weight, out_back), ("z",))
    y_parts[0] = after(y_parts[0], weight_grads)
    pieces = total(col, y_parts)
    in_back, pieces = lax.optimization_barrier((in_back, pieces))
    dx_part = join_in(place, in_back)
    pieces = spread(pieces, EX)
    layer_out, input_grad = last(col, pieces, swap(dx_part, ("z", "xh", "y")))
    return layer_out, input_grad, *weight_grads


def solution(mesh):
    fine = Mesh(mesh.devices.reshape(8, 2, 2, 2, 4), ("z", "xl", "core", "xh", "y"))
    rows, every = P(DP, None), P(DP + EX, None)
    half = P(DP + EX, None, None)
    return jax.shard_map(
        on_device,
        mesh=fine,
        in_specs=(rows, rows, rows, P(), half, half, half, rows),
        out_specs=(every, every, half, half, half),
        check_vma=False,
    )
```
